32 devices in a mesh: wave: 16 (over z, y, core), lev: 2 (over x).
Axes of the slice: x: 2, y: 2, z: 4, core: 2. Of those that a mesh axis runs over, the one named last changes fastest.
Arguments:
- spectral: bfloat16 [6, 2, 2, 640, 640], P('lev', None, None, 'wave'), may hold values from -0.0059814453 to 0.0059814453
- legendre: bfloat16 [640, 1280, 640], P('wave', 'lev'), may hold values from -6 to 6
- thickness: float32 [6], replicated, may hold values from 0.03 to 0.3
- pressure_step: float32 [6], replicated, may hold values from 0.03 to 0.3
- wave_order: int32 [640], replicated, may hold values from 0 to 639, as said below
- lat_order: int32 [1280], replicated, may hold values from 0 to 1279, each once
Outputs:
- spectral_out: float32 [6, 2, 2, 640, 640], P('lev', None, None, 'wave')
The draws below stay inside these ranges and needn't reach their ends.
Inputs may be any that keep to these rules, and one draw needn't show every extreme that they name: `wave_order`: slots 2 p and 2 p + 1 hold the wavenumbers w and 639 - w for some w < 320, the smaller first; every wavenumber appears once. `lat_order`: every latitude index appears once.
All inputs are finite; a program needn't handle non-finite values.
Results may differ from the reference program's by a relative error of at most 0.0046.
Values may be sent and summed in bfloat16 or wider, within the bound.
A program may use at most 128 MiB of HBM per device.

```python
import math
import jax
import jax.numpy as jnp
from jax import lax

M = 640
NLAT = 1280
NLON = 2560
LEV = 6
N_WAVE = 16


def draw_wave_order(key, part):
    pair_ids = jax.random.permutation(key, M // 2).astype(jnp.int32)
    high_ids = M - 1 - pair_ids
    stacked = jnp.stack([pair_ids, high_ids], axis=1)
    return stacked.reshape(M).astype(jnp.int32)


def shard_levels(rng, dims, pieces, low, top_value):
    def one(dim, blocks):
        heights = jax.random.uniform(jax.random.fold_in(jax.random.fold_in(rng, 6), dim), (blocks,), jnp.float32, low / len(pieces), top_value / len(pieces))
        return jnp.repeat(jnp.exp(heights), dims[dim] // blocks).reshape((-1,) + (1,) * (len(dims) - dim - 1))

    level = one(*pieces[0])
    for cut in pieces[1:]:
        level = level * one(*cut)
    return level


def gaussian(own_key, shape, deviation, most, cuts=(), held_as=jnp.bfloat16):
    entries = deviation * jax.random.normal(own_key, shape, jnp.float32)
    if cuts:
        entries = entries * shard_levels(own_key, shape, cuts, -0.22, 0.18)
    return jnp.clip(entries, -most, most).astype(held_as)


def setup_inputs(seed: int = 0) -> dict:
    key_of = jax.random.split(jax.random.key(seed), 7)
    return {
        "spectral": gaussian(key_of[0], (LEV, 2, 2, M, M), 0.001, 0.0059814453, ((0, 2), (3, 16))),
        "legendre": gaussian(key_of[1], (M, NLAT, M), 1.0, 6.0, ((0, 16), (1, 2))),
        "thickness": jnp.clip(jnp.exp(jax.random.uniform(key_of[2], (LEV,), jnp.float32, math.log(0.03), math.log(0.3))), 0.03, 0.3),
        "pressure_step": jnp.clip(jnp.exp(jax.random.uniform(key_of[3], (LEV,), jnp.float32, math.log(0.03), math.log(0.3))), 0.03, 0.3),
        "wave_order": draw_wave_order(jax.random.fold_in(key_of[6], 71), 0),
        "lat_order": jax.random.permutation(key_of[5], NLAT).astype(jnp.int32),
    }


def wave_tables(wave_list, lon_total):
    lon_ids = jnp.arange(lon_total, dtype=jnp.int32)
    phases = (wave_list[:, None] * lon_ids[None, :]) % lon_total
    angles = phases.astype(jnp.float32) * (2.0 * math.pi / lon_total)
    cosine = jnp.cos(angles)
    sine_part = jnp.sin(angles)
    weights = jnp.where(wave_list == 0, 1.0, 2.0).astype(jnp.float32)[:, None]
    inverse = jnp.stack([weights * cosine, -(weights * sine_part)], axis=0).astype(jnp.bfloat16)
    factor = 2.0 / lon_total
    direct = jnp.stack([factor * cosine, -(factor * sine_part)], axis=0)
    direct = jnp.transpose(direct, (2, 0, 1)).astype(jnp.bfloat16)
    return inverse, direct


def mix_levels(temper, diverg, geopot, omega_vel, sin_lat):
    first_field = geopot + omega_vel * temper
    second_field = sin_lat[None, :, None] * omega_vel + diverg * temper
    return jnp.stack([first_field, second_field], axis=1).astype(jnp.bfloat16)


def reference(spectral, legendre, thickness, pressure_step, wave_order, lat_order):
    row_ids = jnp.arange(M, dtype=jnp.int32)
    in_triangle = row_ids[None, :] < (M - wave_order)[:, None]
    inverse_table, forward_legendre_table = wave_tables(wave_order, NLON)
    inverse_wide = inverse_table.astype(jnp.float32)
    forward_wide_rows = forward_legendre_table.astype(jnp.float32)
    angles = math.pi * (lat_order.astype(jnp.float32) + 0.75) / (NLAT + 0.5)
    sin_lat = jnp.cos(angles)
    cos_lat = jnp.sin(angles)

    def inverse_slot(operands):
        spec_slot, leg_slot, mask_slot = operands
        masked = jnp.where(mask_slot[None, :], leg_slot, jnp.zeros((), leg_slot.dtype))
        return jnp.einsum("lfck,qk->lfcq", spec_slot.astype(jnp.float32), masked.astype(jnp.float32)).astype(jnp.bfloat16)

    fourier = lax.map(inverse_slot, (jnp.moveaxis(spectral, 3, 0), legendre, in_triangle))
    fourier = jnp.moveaxis(fourier, 0, 3)
    latitude_block = NLAT // N_WAVE
    block_count = NLAT // latitude_block
    fourier_blocks = jnp.moveaxis(fourier.reshape(LEV, 2, 2, M, block_count, latitude_block), 4, 0)

    def gridpoint_block(operands):
        four_blk, sin_blk, cosine_block = operands
        grid_vals = jnp.einsum("lfcsq,cst->lfqt", four_blk.astype(jnp.float32), inverse_wide)
        temper = grid_vals[:, 0]
        diverg = grid_vals[:, 1]
        geopot = jnp.flip(jnp.cumsum(jnp.flip(thickness[:, None, None] * temper, 0), axis=0), 0)
        omega_vel = -jnp.cumsum(pressure_step[:, None, None] * diverg, axis=0)
        tendency_field = mix_levels(temper, diverg, geopot, omega_vel, sin_blk)
        returned_grid_values = jnp.einsum("opgu,ukh->opkhg", tendency_field.astype(jnp.float32), forward_wide_rows) * cosine_block
        return returned_grid_values.astype(jnp.bfloat16)

    back_blocks = lax.map(gridpoint_block, (fourier_blocks, sin_lat.reshape(block_count, latitude_block), cos_lat.reshape(block_count, latitude_block)))
    back_full = jnp.moveaxis(back_blocks, 0, 4).reshape(LEV, 2, 2, M, NLAT)

    def direct_slot(operands):
        back_slot, leg_slot, mask_slot = operands
        masked = jnp.where(mask_slot[None, :], leg_slot, jnp.zeros((), leg_slot.dtype))
        return jnp.einsum("lfcq,qk->lfck", back_slot.astype(jnp.float32), masked.astype(jnp.float32))

    result = lax.map(direct_slot, (jnp.moveaxis(back_full, 3, 0), legendre, in_triangle))
    return jnp.moveaxis(result, 0, 3)
```

```python
import math

import jax
import jax.numpy as jnp
from jax import lax
from jax.experimental import pallas as pl
from jax.experimental.pallas import tpu as pltpu
from jax.sharding import PartitionSpec as P

M = 640
NLAT = 1280
NLON = 2560


def wave_tables(wave_list, lon_total):
    lon_ids = jnp.arange(lon_total, dtype=jnp.int32)
    phases = wave_list[:, None] * lon_ids[None, :] % lon_total
    angles = phases.astype(jnp.float32) * (2.0 * math.pi / lon_total)
    cosine = jnp.cos(angles)
    sine_part = jnp.sin(angles)
    weights = jnp.where(wave_list == 0, 1.0, 2.0).astype(jnp.float32)[:, None]
    inverse = jnp.stack([weights * cosine, -(weights * sine_part)], axis=0).astype(jnp.bfloat16)
    factor = 2.0 / lon_total
    direct = jnp.stack([factor * cosine, -(factor * sine_part)], axis=0)
    direct = jnp.transpose(direct, (2, 0, 1)).astype(jnp.bfloat16)
    return (inverse, direct)


def mix_levels(temper, diverg, geopot, omega_vel, sin_lat):
    first_field = geopot + omega_vel * temper
    second_field = sin_lat[None, :, None] * omega_vel + diverg * temper
    return jnp.stack([first_field, second_field], axis=1).astype(jnp.bfloat16)


def general_body(spectral, legendre, thickness, pressure_step, wave_order, lat_order):
    wave_index = lax.axis_index("wave")
    wave_count = lax.axis_size("wave")
    local_slots = legendre.shape[0]
    grid_lats = NLAT // wave_count
    my_waves = lax.dynamic_slice(wave_order, (wave_index * local_slots,), (local_slots,))
    row_ids = jnp.arange(M, dtype=jnp.int32)
    in_triangle = row_ids[None, :] < (M - my_waves)[:, None]
    masked_leg = jnp.where(in_triangle[:, None, :], legendre, jnp.zeros((), jnp.bfloat16))
    fourier = jnp.einsum(
        "lfcsk,sqk->lfcsq",
        lax.all_gather(spectral, "lev", axis=0, tiled=True),
        masked_leg,
        preferred_element_type=jnp.float32,
    ).astype(jnp.bfloat16)
    level_split = lax.all_to_all(fourier, "lev", split_axis=0, concat_axis=4, tiled=True)
    inverse_table, forward_legendre_table = wave_tables(wave_order, NLON)
    grid_vals = jnp.einsum(
        "lfcsq,cst->lfqt",
        lax.all_to_all(level_split, "wave", split_axis=4, concat_axis=3, tiled=True),
        inverse_table,
        preferred_element_type=jnp.float32,
    )
    lat_ids = lax.dynamic_slice(lat_order, (wave_index * grid_lats,), (grid_lats,))
    angles = math.pi * (lat_ids.astype(jnp.float32) + 0.75) / (NLAT + 0.5)
    sin_lat = jnp.cos(angles)
    cos_lat = jnp.sin(angles)
    columns = lax.all_to_all(grid_vals, "lev", split_axis=3, concat_axis=0, tiled=True)
    temper = columns[:, 0]
    diverg = columns[:, 1]
    geopot = jnp.flip(jnp.cumsum(jnp.flip(thickness[:, None, None] * temper, 0), axis=0), 0)
    omega_vel = -jnp.cumsum(pressure_step[:, None, None] * diverg, axis=0)
    tend_cols = mix_levels(temper, diverg, geopot, omega_vel, sin_lat)
    tendency_field = lax.all_to_all(tend_cols, "lev", split_axis=0, concat_axis=3, tiled=True)
    returned_grid_values = (
        jnp.einsum(
            "opgu,ukh->opkhg",
            tendency_field,
            forward_legendre_table,
            preferred_element_type=jnp.float32,
        )
        * cos_lat
    ).astype(jnp.bfloat16)
    band_vals = lax.all_to_all(
        lax.all_to_all(returned_grid_values, "wave", split_axis=3, concat_axis=4, tiled=True),
        "lev",
        split_axis=4,
        concat_axis=0,
        tiled=True,
    )
    summed = lax.psum_scatter(
        jnp.einsum("lfcsq,sqk->lfcsk", band_vals, masked_leg, preferred_element_type=jnp.float32),
        "lev",
        scatter_dimension=0,
        tiled=True,
    )
    return summed


LANES = 128
ROWS = 256
VMEM_LIMIT = 48 * 1024 * 1024


def placed(rows, cols, row_start, col_start, count):
    r = lax.broadcasted_iota(jnp.int32, (rows, cols), 0)
    c = lax.broadcasted_iota(jnp.int32, (rows, cols), 1)
    hit = (r - row_start == c - col_start) & (c >= col_start) & (c < col_start + count)
    return jnp.where(hit, 1.0, 0.0).astype(jnp.bfloat16)


def inverse_legendre_kernel(slots, lats, lv, nw, spec_ref, leg_ref, out_ref, cut, held):
    s = pl.program_id(0)
    tiles = cut.shape[0]

    @pl.when(s == 0)
    def _():
        for b in range(tiles):
            cut[b] = spec_ref[:, b * LANES : (b + 1) * LANES]

    x = jnp.concatenate([cut[b, pl.ds(s, 8 * lv, stride=slots), :] for b in range(tiles)], axis=1).astype(jnp.bfloat16)
    y = lax.dot_general(x, leg_ref[0], (((1,), (1,)), ((), ())), preferred_element_type=jnp.float32)
    blocks = y.shape[1] // LANES
    for l in range(lv):
        for b in range(blocks):
            held[l * blocks + b, pl.ds(s, 8, stride=slots), :] = y[8 * l : 8 * l + 8, b * LANES : (b + 1) * LANES]

    @pl.when(s == slots - 1)
    def _():
        for d in range(nw):
            total = jnp.zeros((8 * slots, LANES), jnp.float32)
            for b in range(lats * d // LANES, (lats * (d + 1) - 1) // LANES + 1):
                for l in range(lv):
                    first = max(lats * d, LANES * b)
                    last = min(lats * (d + 1), LANES * (b + 1))
                    sel = placed(LANES, LANES, first - LANES * b, lats * l + first - lats * d, last - first)
                    total += jnp.dot(held[l * blocks + b].astype(jnp.bfloat16), sel, preferred_element_type=jnp.float32)
            out_ref[d] = total.astype(jnp.bfloat16)


def inverse_legendre(spec, legendre, lv, nw):
    slots, band, rows = legendre.shape
    lats = band // nw
    return pl.pallas_call(
        lambda *refs: inverse_legendre_kernel(slots, lats, lv, nw, *refs),
        grid=(slots,),
        in_specs=[
            pl.BlockSpec((8 * lv * slots, rows), lambda s: (0, 0)),
            pl.BlockSpec((1, band, rows), lambda s: (s, 0, 0)),
        ],
        out_specs=pl.BlockSpec((nw, 8 * slots, LANES), lambda s: (0, 0, 0)),
        out_shape=jax.ShapeDtypeStruct((nw, 8 * slots, LANES), jnp.bfloat16),
        scratch_shapes=[
            pltpu.VMEM((rows // LANES, 8 * lv * slots, LANES), jnp.float32),
            pltpu.VMEM((lv * band // LANES, 8 * slots, LANES), jnp.float32),
        ],
        compiler_params=pltpu.CompilerParams(vmem_limit_bytes=VMEM_LIMIT),
        cost_estimate=pl.CostEstimate(flops=2 * slots * band * rows * 256, bytes_accessed=2 * slots * band * rows, transcendentals=0),
        name="inverse_legendre",
    )(spec, legendre)


def grid_kernel(steps, factor, recv_ref, cos_ref, sin_ref, row_ref, lane_ref, down_ref, up_ref, out_ref, operand, total):
    i = pl.program_id(0)
    half = recv_ref.shape[1] // 4
    nw = recv_ref.shape[0]

    @pl.when(i == 0)
    def _():
        for j in range(4):
            operand[:, j * LANES : (j + 1) * LANES] = recv_ref[:, j * half : (j + 1) * half, :].reshape(nw * half, LANES)

    parts = []
    for u in range(ROWS // LANES):
        row = row_ref[i * (ROWS // LANES) + u]
        parts.append(cos_ref[...] * row[0:1, :] - sin_ref[...] * row[1:2, :])
    table = jnp.concatenate(parts, axis=0)
    values = jnp.dot(table.astype(jnp.bfloat16), operand[...], preferred_element_type=jnp.float32)
    temper = values[:, : 2 * LANES]
    diverg = values[:, 2 * LANES :]

    def level_sum(x, matrix):
        high = x.astype(jnp.bfloat16)
        low = (x - high.astype(jnp.float32)).astype(jnp.bfloat16)
        return jnp.dot(high, matrix, preferred_element_type=jnp.float32) + jnp.dot(low, matrix, preferred_element_type=jnp.float32)

    geopot = level_sum(temper * lane_ref[0:1, :], up_ref[...])
    omega = -level_sum(diverg * lane_ref[1:2, :], down_ref[...])
    first = geopot + omega * temper
    second = lane_ref[2:3, :] * omega + diverg * temper
    tendency = jnp.concatenate([first, second], axis=1).astype(jnp.bfloat16)
    part = lax.dot_general((table * factor).astype(jnp.bfloat16), tendency, (((0,), (0,)), ((), ())), preferred_element_type=jnp.float32)

    @pl.when(i == 0)
    def _():
        total[...] = part

    @pl.when(i > 0)
    def _():
        total[...] += part

    @pl.when(i == steps - 1)
    def _():
        scale = lane_ref[3:4, :]
        out_ref[...] = (total[...] * jnp.concatenate([scale, scale], axis=1)).astype(jnp.bfloat16)


def grid_space(recv, cos_base, sin_base, row_table, lane_values, down, up):
    steps = NLON // ROWS
    waves = cos_base.shape[1]
    whole = lambda a: pl.BlockSpec(a.shape, lambda i, n=a.ndim: (0,) * n)
    args = (recv, cos_base, sin_base, row_table, lane_values, down, up)
    return pl.pallas_call(
        lambda *refs: grid_kernel(steps, 2.0 / NLON, *refs),
        grid=(steps,),
        in_specs=[whole(a) for a in args],
        out_specs=pl.BlockSpec((waves, 4 * LANES), lambda i: (0, 0)),
        out_shape=jax.ShapeDtypeStruct((waves, 4 * LANES), jnp.bfloat16),
        scratch_shapes=[pltpu.VMEM((waves, 4 * LANES), jnp.bfloat16), pltpu.VMEM((waves, 4 * LANES), jnp.float32)],
        compiler_params=pltpu.CompilerParams(vmem_limit_bytes=VMEM_LIMIT),
        cost_estimate=pl.CostEstimate(flops=4 * NLON * waves * 4 * LANES, bytes_accessed=8 * waves * LANES, transcendentals=0),
        name="grid_space",
    )(*args)


def direct_legendre_kernel(slots, lats, lv, wave_ref, recv_ref, leg_ref, out_ref, held, cut):
    s = pl.program_id(0)
    nw = recv_ref.shape[0]
    blocks = leg_ref.shape[1] // LANES

    @pl.when(s == 0)
    def _():
        for b in range(blocks):
            total = jnp.zeros((8 * slots, lv * LANES), jnp.float32)
            for w in range(LANES * b // lats, (LANES * (b + 1) - 1) // lats + 1):
                first = max(lats * w, LANES * b)
                last = min(lats * (w + 1), LANES * (b + 1))
                x = jnp.concatenate([recv_ref[w, :, j * LANES : (j + 1) * LANES] for j in range(4)], axis=0)
                sel = jnp.concatenate(
                    [placed(LANES, LANES, lats * l + first - lats * w, first - LANES * b, last - first) for l in range(lv)], axis=1
                )
                total += jnp.dot(x, sel, preferred_element_type=jnp.float32)
            for l in range(lv):
                held[l * blocks + b] = total[:, l * LANES : (l + 1) * LANES]

    x = jnp.concatenate(
        [jnp.concatenate([held[l * blocks + b, pl.ds(s, 8, stride=slots), :] for b in range(blocks)], axis=1) for l in range(lv)], axis=0
    ).astype(jnp.bfloat16)
    y = jnp.dot(x, leg_ref[0], preferred_element_type=jnp.float32)
    k = lax.broadcasted_iota(jnp.int32, y.shape, 1)
    y = jnp.where(k < M - wave_ref[s], y, 0.0)
    for b in range(cut.shape[0]):
        cut[b, pl.ds(s, 8 * lv, stride=slots), :] = y[:, b * LANES : (b + 1) * LANES]

    @pl.when(s == slots - 1)
    def _():
        for b in range(cut.shape[0]):
            out_ref[:, b * LANES : (b + 1) * LANES] = cut[b]


def direct_legendre(my_waves, recv, legendre, lv):
    slots, band, rows = legendre.shape
    nw = recv.shape[0]
    return pl.pallas_call(
        lambda *refs: direct_legendre_kernel(slots, band // nw, lv, *refs),
        grid_spec=pltpu.PrefetchScalarGridSpec(
            num_scalar_prefetch=1,
            grid=(slots,),
            in_specs=[
                pl.BlockSpec(recv.shape, lambda s, w: (0, 0, 0)),
                pl.BlockSpec((1, band, rows), lambda s, w: (s, 0, 0)),
            ],
            out_specs=pl.BlockSpec((8 * lv * slots, rows), lambda s, w: (0, 0)),
            scratch_shapes=[
                pltpu.VMEM((lv * band // LANES, 8 * slots, LANES), jnp.float32),
                pltpu.VMEM((rows // LANES, 8 * lv * slots, LANES), jnp.float32),
            ],
        ),
        out_shape=jax.ShapeDtypeStruct((8 * lv * slots, rows), jnp.float32),
        compiler_params=pltpu.CompilerParams(vmem_limit_bytes=VMEM_LIMIT),
        cost_estimate=pl.CostEstimate(flops=2 * slots * band * rows * 256, bytes_accessed=2 * slots * band * rows, transcendentals=0),
        name="direct_legendre",
    )(my_waves, recv, legendre)


def body(spectral, legendre, thickness, pressure_step, wave_order, lat_order):
    wave_index = lax.axis_index("wave")
    lev_index = lax.axis_index("lev")
    nw = lax.axis_size("wave")
    slots, band, rows = legendre.shape
    lats = band // nw
    lv = spectral.shape[0]
    swap = [(0, 1), (1, 0)]
    upper = lev_index == 0

    other = lax.ppermute(spectral, "lev", swap)
    my_waves = lax.dynamic_slice(wave_order, (wave_index * slots,), (slots,))
    in_triangle = jnp.arange(rows, dtype=jnp.int32)[None, :] < (M - my_waves)[:, None]
    weights = jnp.where(my_waves == 0, 1.0, 2.0).astype(jnp.float32)[:, None]
    weights = jnp.where(in_triangle, weights, 0.0)

    lane_waves = jnp.broadcast_to(wave_order.reshape(nw, 1, slots), (nw, 2, slots)).reshape(1, -1)
    turn = 2.0 * math.pi / NLON
    inner = (lane_waves * jnp.arange(LANES, dtype=jnp.int32)[:, None] % NLON).astype(jnp.float32) * turn
    cos_base, sin_base = jnp.cos(inner), jnp.sin(inner)
    outer = (lane_waves * jnp.arange(0, NLON, LANES, dtype=jnp.int32)[:, None] % NLON).astype(jnp.float32) * turn
    imaginary = (jnp.arange(2 * nw * slots) // slots % 2 == 1)[None, :]
    cos_outer, sin_outer = jnp.cos(outer), jnp.sin(outer)
    row_table = jnp.stack([jnp.where(imaginary, -sin_outer, cos_outer), jnp.where(imaginary, cos_outer, sin_outer)], axis=1)

    lat_ids = lax.dynamic_slice(lat_order, (lev_index * band + wave_index * lats,), (lats,))
    angles = math.pi * (lat_ids.astype(jnp.float32) + 0.75) / (NLAT + 0.5)

    def lanes(by_level_lat):
        pad = LANES - lv * lats
        return jnp.pad(by_level_lat.reshape(2, lv * lats), ((0, 0), (0, pad))).reshape(2 * LANES)

    spread = jnp.ones((2 * lv, lats), jnp.float32)
    zero = jnp.zeros((2 * LANES,), jnp.float32)
    lane_values = jnp.stack(
        [lanes(thickness[:, None] * spread), lanes(pressure_step[:, None] * spread), lanes(jnp.cos(angles) * spread), lanes(jnp.sin(angles) * spread)]
        + [zero] * 4
    )
    place = jnp.arange(2 * LANES)
    valid = place % LANES < lv * lats
    level = place // LANES * lv + place % LANES // lats
    lat = place % LANES % lats
    same = (lat[:, None] == lat[None, :]) & valid[:, None] & valid[None, :]
    down = (same & (level[:, None] <= level[None, :])).astype(jnp.bfloat16)
    up = (same & (level[:, None] >= level[None, :])).astype(jnp.bfloat16)

    halves = jnp.stack([jnp.where(upper, spectral, other), jnp.where(upper, other, spectral)], axis=2)
    spec = (halves.astype(jnp.float32) * weights).reshape(8 * lv * slots, rows)
    sent = inverse_legendre(spec, legendre, lv, nw)
    recv = lax.all_to_all(sent, "wave", split_axis=0, concat_axis=0, tiled=True)
    back = grid_space(recv, cos_base, sin_base, row_table, lane_values, down, up)
    back = lax.all_to_all(back.reshape(nw, 2 * slots, 4 * LANES), "wave", split_axis=0, concat_axis=0, tiled=True)
    out = direct_legendre(my_waves, back, legendre, lv).reshape(lv, 2, 2, 2, slots, rows)
    mine = jnp.where(upper, out[:, :, 0], out[:, :, 1])
    theirs = jnp.where(upper, out[:, :, 1], out[:, :, 0]).astype(jnp.bfloat16)
    return mine + lax.ppermute(theirs, "lev", swap).astype(jnp.float32)


def solution(mesh):
    nw, nl = mesh.shape["wave"], mesh.shape["lev"]

    def run(spectral, *rest):
        slots, lv = M // nw, spectral.shape[0] // nl
        fits = nl == 2 and NLAT % (nw * nl) == 0 and M % nw == 0 and slots % 8 == 0
        fits = fits and M % LANES == 0 and lv * (NLAT // (nw * nl)) <= LANES and (NLAT // nl) % LANES == 0
        in_specs = (P("lev", None, None, "wave", None), P("wave", "lev", None), P(), P(), P(), P())
        out_specs = P("lev", None, None, "wave", None)
        chosen = body if fits else general_body
        return jax.shard_map(chosen, mesh=mesh, in_specs=in_specs, out_specs=out_specs, check_vma=False)(spectral, *rest)

    return run
```

```python
import math

import jax
import jax.numpy as jnp
from jax import lax
from jax.experimental import pallas as pl
from jax.experimental.pallas import tpu as pltpu
from jax.sharding import PartitionSpec as P

M = 640
NLAT = 1280
NLON = 2560


def wave_tables(wave_list, lon_total):
    lon_ids = jnp.arange(lon_total, dtype=jnp.int32)
    phases = wave_list[:, None] * lon_ids[None, :] % lon_total
    angles = phases.astype(jnp.float32) * (2.0 * math.pi / lon_total)
    cosine = jnp.cos(angles)
    sine_part = jnp.sin(angles)
    weights = jnp.where(wave_list == 0, 1.0, 2.0).astype(jnp.float32)[:, None]
    inverse = jnp.stack([weights * cosine, -(weights * sine_part)], axis=0).astype(jnp.bfloat16)
    factor = 2.0 / lon_total
    direct = jnp.stack([factor * cosine, -(factor * sine_part)], axis=0)
    direct = jnp.transpose(direct, (2, 0, 1)).astype(jnp.bfloat16)
    return (inverse, direct)


def mix_levels(temper, diverg, geopot, omega_vel, sin_lat):
    first_field = geopot + omega_vel * temper
    second_field = sin_lat[None, :, None] * omega_vel + diverg * temper
    return jnp.stack([first_field, second_field], axis=1).astype(jnp.bfloat16)


def general_body(spectral, legendre, thickness, pressure_step, wave_order, lat_order):
    wave_index = lax.axis_index("wave")
    wave_count = lax.axis_size("wave")
    local_slots = legendre.shape[0]
    grid_lats = NLAT // wave_count
    my_waves = lax.dynamic_slice(wave_order, (wave_index * local_slots,), (local_slots,))
    row_ids = jnp.arange(M, dtype=jnp.int32)
    in_triangle = row_ids[None, :] < (M - my_waves)[:, None]
    masked_leg = jnp.where(in_triangle[:, None, :], legendre, jnp.zeros((), jnp.bfloat16))
    fourier = jnp.einsum(
        "lfcsk,sqk->lfcsq",
        lax.all_gather(spectral, "lev", axis=0, tiled=True),
        masked_leg,
        preferred_element_type=jnp.float32,
    ).astype(jnp.bfloat16)
    level_split = lax.all_to_all(fourier, "lev", split_axis=0, concat_axis=4, tiled=True)
    inverse_table, forward_legendre_table = wave_tables(wave_order, NLON)
    grid_vals = jnp.einsum(
        "lfcsq,cst->lfqt",
        lax.all_to_all(level_split, "wave", split_axis=4, concat_axis=3, tiled=True),
        inverse_table,
        preferred_element_type=jnp.float32,
    )
    lat_ids = lax.dynamic_slice(lat_order, (wave_index * grid_lats,), (grid_lats,))
    angles = math.pi * (lat_ids.astype(jnp.float32) + 0.75) / (NLAT + 0.5)
    sin_lat = jnp.cos(angles)
    cos_lat = jnp.sin(angles)
    columns = lax.all_to_all(grid_vals, "lev", split_axis=3, concat_axis=0, tiled=True)
    temper = columns[:, 0]
    diverg = columns[:, 1]
    geopot = jnp.flip(jnp.cumsum(jnp.flip(thickness[:, None, None] * temper, 0), axis=0), 0)
    omega_vel = -jnp.cumsum(pressure_step[:, None, None] * diverg, axis=0)
    tend_cols = mix_levels(temper, diverg, geopot, omega_vel, sin_lat)
    tendency_field = lax.all_to_all(tend_cols, "lev", split_axis=0, concat_axis=3, tiled=True)
    returned_grid_values = (
        jnp.einsum(
            "opgu,ukh->opkhg",
            tendency_field,
            forward_legendre_table,
            preferred_element_type=jnp.float32,
        )
        * cos_lat
    ).astype(jnp.bfloat16)
    band_vals = lax.all_to_all(
        lax.all_to_all(returned_grid_values, "wave", split_axis=3, concat_axis=4, tiled=True),
        "lev",
        split_axis=4,
        concat_axis=0,
        tiled=True,
    )
    summed = lax.psum_scatter(
        jnp.einsum("lfcsq,sqk->lfcsk", band_vals, masked_leg, preferred_element_type=jnp.float32),
        "lev",
        scatter_dimension=0,
        tiled=True,
    )
    return summed


LANES = 128
ROWS = 256
UNROLL = 4
VMEM_LIMIT = 48 * 1024 * 1024


def placed(rows, cols, row_start, col_start, count):
    r = lax.broadcasted_iota(jnp.int32, (rows, cols), 0)
    c = lax.broadcasted_iota(jnp.int32, (rows, cols), 1)
    hit = (r - row_start == c - col_start) & (c >= col_start) & (c < col_start + count)
    return jnp.where(hit, 1.0, 0.0).astype(jnp.bfloat16)


def inverse_legendre_kernel(slots, lats, lv, nw, spec_ref, leg_ref, out_ref, cut, held):
    step = pl.program_id(0)
    tiles = cut.shape[0]
    count = 8 * lv

    @pl.when(step == 0)
    def _():
        for b in range(tiles):
            cut[b] = spec_ref[:, b * LANES : (b + 1) * LANES]

    total = None
    for j in range(UNROLL):
        x = jnp.concatenate([cut[b, pl.ds(step * UNROLL + j, count, stride=slots), :] for b in range(tiles)], axis=1)
        x = jnp.concatenate([x if i == j else jnp.zeros_like(x) for i in range(UNROLL)], axis=0).astype(jnp.bfloat16)
        part = lax.dot_general(leg_ref[j], x, (((1,), (1,)), ((), ())), preferred_element_type=jnp.float32)
        total = part if total is None else total + part
    y = total.T
    blocks = y.shape[1] // LANES
    for j in range(UNROLL):
        for l in range(lv):
            for b in range(blocks):
                r = count * j + 8 * l
                held[l * blocks + b, pl.ds(step * UNROLL + j, 8, stride=slots), :] = y[r : r + 8, b * LANES : (b + 1) * LANES]

    @pl.when(step == slots // UNROLL - 1)
    def _():
        for d in range(nw):
            total = jnp.zeros((8 * slots, LANES), jnp.float32)
            for b in range(lats * d // LANES, (lats * (d + 1) - 1) // LANES + 1):
                for l in range(lv):
                    first = max(lats * d, LANES * b)
                    last = min(lats * (d + 1), LANES * (b + 1))
                    sel = placed(LANES, LANES, first - LANES * b, lats * l + first - lats * d, last - first)
                    total += jnp.dot(held[l * blocks + b].astype(jnp.bfloat16), sel, preferred_element_type=jnp.float32)
            out_ref[d] = total.astype(jnp.bfloat16)


def inverse_legendre(spec, legendre, start, slots, lv, nw):
    _, band, rows = legendre.shape
    lats = band // nw
    return pl.pallas_call(
        lambda *refs: inverse_legendre_kernel(slots, lats, lv, nw, *refs),
        grid=(slots // UNROLL,),
        in_specs=[
            pl.BlockSpec((8 * lv * slots, rows), lambda s: (0, 0)),
            pl.BlockSpec((UNROLL, band, rows), lambda s: (s + start // UNROLL, 0, 0)),
        ],
        out_specs=pl.BlockSpec((nw, 8 * slots, LANES), lambda s: (0, 0, 0)),
        out_shape=jax.ShapeDtypeStruct((nw, 8 * slots, LANES), jnp.bfloat16),
        scratch_shapes=[
            pltpu.VMEM((rows // LANES, 8 * lv * slots, LANES), jnp.float32),
            pltpu.VMEM((lv * band // LANES, 8 * slots, LANES), jnp.float32),
        ],
        compiler_params=pltpu.CompilerParams(vmem_limit_bytes=VMEM_LIMIT),
        cost_estimate=pl.CostEstimate(flops=2 * slots * band * rows * 256, bytes_accessed=2 * slots * band * rows, transcendentals=0),
        name="inverse_legendre",
    )(spec, legendre)


def grid_kernel(steps, factor, groups, *refs):
    i = pl.program_id(0)
    recvs, (cos_ref, sin_ref, row_ref, lane_ref, down_ref, up_ref) = refs[:groups], refs[groups : groups + 6]
    outs, (operand, total) = refs[groups + 6 : -2], refs[-2:]

    @pl.when(i == 0)
    def _():
        top = 0
        for recv in recvs:
            nw, half = recv.shape[0], recv.shape[1] // 4
            for j in range(4):
                operand[top : top + nw * half, j * LANES : (j + 1) * LANES] = recv[:, j * half : (j + 1) * half, :].reshape(nw * half, LANES)
            top += nw * half

    parts = []
    for u in range(ROWS // LANES):
        row = row_ref[i * (ROWS // LANES) + u]
        parts.append(cos_ref[...] * row[0:1, :] - sin_ref[...] * row[1:2, :])
    table = jnp.concatenate(parts, axis=0)
    values = jnp.dot(table.astype(jnp.bfloat16), operand[...], preferred_element_type=jnp.float32)
    temper = values[:, : 2 * LANES]
    diverg = values[:, 2 * LANES :]

    def level_sum(x, matrix):
        high = x.astype(jnp.bfloat16)
        low = (x - high.astype(jnp.float32)).astype(jnp.bfloat16)
        return jnp.dot(high, matrix, preferred_element_type=jnp.float32) + jnp.dot(low, matrix, preferred_element_type=jnp.float32)

    geopot = level_sum(temper * lane_ref[0:1, :], up_ref[...])
    omega = -level_sum(diverg * lane_ref[1:2, :], down_ref[...])
    first = geopot + omega * temper
    second = lane_ref[2:3, :] * omega + diverg * temper
    tendency = jnp.concatenate([first, second], axis=1).astype(jnp.bfloat16)
    part = lax.dot_general((table * factor).astype(jnp.bfloat16), tendency, (((0,), (0,)), ((), ())), preferred_element_type=jnp.float32)

    @pl.when(i == 0)
    def _():
        total[...] = part

    @pl.when(i > 0)
    def _():
        total[...] += part

    @pl.when(i == steps - 1)
    def _():
        scale = lane_ref[3:4, :]
        scale = jnp.concatenate([scale, scale], axis=1)
        top = 0
        for out in outs:
            nw, half = out.shape[0], out.shape[1] // 4
            for j in range(4):
                lanes = slice(j * LANES, (j + 1) * LANES)
                block = (total[top : top + nw * half, lanes] * scale[:, lanes]).astype(jnp.bfloat16)
                out[:, j * half : (j + 1) * half, :] = block.reshape(nw, half, LANES)
            top += nw * half


def grid_space(recvs, *tables):
    steps = NLON // ROWS
    waves = tables[0].shape[1]
    whole = lambda a: pl.BlockSpec(a.shape, lambda i, n=a.ndim: (0,) * n)
    args = (*recvs, *tables)
    return pl.pallas_call(
        lambda *refs: grid_kernel(steps, 2.0 / NLON, len(recvs), *refs),
        grid=(steps,),
        in_specs=[whole(a) for a in args],
        out_specs=[whole(a) for a in recvs],
        out_shape=[jax.ShapeDtypeStruct(a.shape, a.dtype) for a in recvs],
        scratch_shapes=[pltpu.VMEM((waves, 4 * LANES), jnp.bfloat16), pltpu.VMEM((waves, 4 * LANES), jnp.float32)],
        compiler_params=pltpu.CompilerParams(vmem_limit_bytes=VMEM_LIMIT),
        cost_estimate=pl.CostEstimate(flops=4 * NLON * waves * 4 * LANES, bytes_accessed=8 * waves * LANES, transcendentals=0),
        name="grid_space",
    )(*args)


def direct_legendre_kernel(start, slots, lats, lv, wave_ref, recv_ref, leg_ref, out_ref, held, cut):
    step = pl.program_id(0)
    blocks = leg_ref.shape[1] // LANES

    @pl.when(step == 0)
    def _():
        for b in range(blocks):
            total = jnp.zeros((8 * slots, lv * LANES), jnp.float32)
            for w in range(LANES * b // lats, (LANES * (b + 1) - 1) // lats + 1):
                first = max(lats * w, LANES * b)
                last = min(lats * (w + 1), LANES * (b + 1))
                sel = jnp.concatenate(
                    [placed(LANES, LANES, lats * l + first - lats * w, first - LANES * b, last - first) for l in range(lv)], axis=1
                )
                total += jnp.dot(recv_ref[w], sel, preferred_element_type=jnp.float32)
            for l in range(lv):
                held[l * blocks + b] = total[:, l * LANES : (l + 1) * LANES]

    for j in range(UNROLL):
        s = step * UNROLL + j
        x = jnp.concatenate(
            [jnp.concatenate([held[l * blocks + b, pl.ds(s, 8, stride=slots), :] for b in range(blocks)], axis=1) for l in range(lv)], axis=0
        ).astype(jnp.bfloat16)
        y = jnp.dot(x, leg_ref[j], preferred_element_type=jnp.float32)
        k = lax.broadcasted_iota(jnp.int32, y.shape, 1)
        y = jnp.where(k < M - wave_ref[start + s], y, 0.0)
        for b in range(cut.shape[0]):
            cut[b, pl.ds(s, 8 * lv, stride=slots), :] = y[:, b * LANES : (b + 1) * LANES]

    @pl.when(step == slots // UNROLL - 1)
    def _():
        for b in range(cut.shape[0]):
            out_ref[:, b * LANES : (b + 1) * LANES] = cut[b]


def direct_legendre(my_waves, recv, legendre, start, slots, lv):
    _, band, rows = legendre.shape
    nw = recv.shape[0]
    return pl.pallas_call(
        lambda *refs: direct_legendre_kernel(start, slots, band // nw, lv, *refs),
        grid_spec=pltpu.PrefetchScalarGridSpec(
            num_scalar_prefetch=1,
            grid=(slots // UNROLL,),
            in_specs=[
                pl.BlockSpec(recv.shape, lambda s, w: (0, 0, 0)),
                pl.BlockSpec((UNROLL, band, rows), lambda s, w: (s + start // UNROLL, 0, 0)),
            ],
            out_specs=pl.BlockSpec((8 * lv * slots, rows), lambda s, w: (0, 0)),
            scratch_shapes=[
                pltpu.VMEM((lv * band // LANES, 8 * slots, LANES), jnp.float32),
                pltpu.VMEM((rows // LANES, 8 * lv * slots, LANES), jnp.float32),
            ],
        ),
        out_shape=jax.ShapeDtypeStruct((8 * lv * slots, rows), jnp.float32),
        compiler_params=pltpu.CompilerParams(vmem_limit_bytes=VMEM_LIMIT),
        cost_estimate=pl.CostEstimate(flops=2 * slots * band * rows * 256, bytes_accessed=2 * slots * band * rows, transcendentals=0),
        name="direct_legendre",
    )(my_waves, recv, legendre)


def body(spectral, legendre, thickness, pressure_step, wave_order, lat_order):
    wave_index = lax.axis_index("wave")
    lev_index = lax.axis_index("lev")
    nw = lax.axis_size("wave")
    slots, band, rows = legendre.shape
    lats = band // nw
    lv = spectral.shape[0]
    swap = [(0, 1), (1, 0)]
    upper = lev_index == 0

    cutoff = slots * 2 // 5 // 8 * 8
    groups = [(0, cutoff), (cutoff, slots - cutoff)] if cutoff else [(0, slots)]
    own = [spectral[:, :, :, start : start + n] for start, n in groups]
    others = [lax.ppermute(x, "lev", swap) for x in own]
    my_waves = lax.dynamic_slice(wave_order, (wave_index * slots,), (slots,))
    in_triangle = jnp.arange(rows, dtype=jnp.int32)[None, :] < (M - my_waves)[:, None]
    weights = jnp.where(my_waves == 0, 1.0, 2.0).astype(jnp.float32)[:, None]
    weights = jnp.where(in_triangle, weights, 0.0)

    by_device = wave_order.reshape(nw, 1, slots)
    lane_waves = jnp.concatenate(
        [jnp.broadcast_to(by_device[:, :, start : start + n], (nw, 2, n)).reshape(1, -1) for start, n in groups], axis=1
    )
    imaginary = jnp.concatenate([jnp.arange(2 * nw * n) // n % 2 == 1 for _, n in groups])[None, :]
    turn = 2.0 * math.pi / NLON
    inner = (lane_waves * jnp.arange(LANES, dtype=jnp.int32)[:, None] % NLON).astype(jnp.float32) * turn
    cos_base, sin_base = jnp.cos(inner), jnp.sin(inner)
    outer = (lane_waves * jnp.arange(0, NLON, LANES, dtype=jnp.int32)[:, None] % NLON).astype(jnp.float32) * turn
    cos_outer, sin_outer = jnp.cos(outer), jnp.sin(outer)
    row_table = jnp.stack([jnp.where(imaginary, -sin_outer, cos_outer), jnp.where(imaginary, cos_outer, sin_outer)], axis=1)

    lat_ids = lax.dynamic_slice(lat_order, (lev_index * band + wave_index * lats,), (lats,))
    angles = math.pi * (lat_ids.astype(jnp.float32) + 0.75) / (NLAT + 0.5)

    def lanes(by_level_lat):
        pad = LANES - lv * lats
        return jnp.pad(by_level_lat.reshape(2, lv * lats), ((0, 0), (0, pad))).reshape(2 * LANES)

    spread = jnp.ones((2 * lv, lats), jnp.float32)
    zero = jnp.zeros((2 * LANES,), jnp.float32)
    lane_values = jnp.stack(
        [lanes(thickness[:, None] * spread), lanes(pressure_step[:, None] * spread), lanes(jnp.cos(angles) * spread), lanes(jnp.sin(angles) * spread)]
        + [zero] * 4
    )
    place = jnp.arange(2 * LANES)
    valid = place % LANES < lv * lats
    level = place // LANES * lv + place % LANES // lats
    lat = place % LANES % lats
    same = (lat[:, None] == lat[None, :]) & valid[:, None] & valid[None, :]
    down = (same & (level[:, None] <= level[None, :])).astype(jnp.bfloat16)
    up = (same & (level[:, None] >= level[None, :])).astype(jnp.bfloat16)

    recvs = []
    for (start, n), x, other in zip(groups, own, others):
        halves = jnp.stack([jnp.where(upper, x, other), jnp.where(upper, other, x)], axis=2)
        spec = (halves.astype(jnp.float32) * weights[start : start + n]).reshape(8 * lv * n, rows)
        sent = inverse_legendre(spec, legendre, start, n, lv, nw)
        recvs.append(lax.all_to_all(sent, "wave", split_axis=0, concat_axis=0, tiled=True))
    backs = grid_space(recvs, cos_base, sin_base, row_table, lane_values, down, up)
    results = []
    for (start, n), back in reversed(list(zip(groups, backs))):
        back = lax.all_to_all(back, "wave", split_axis=0, concat_axis=0, tiled=True)
        out = direct_legendre(my_waves, back, legendre, start, n, lv).reshape(lv, 2, 2, 2, n, rows)
        mine = jnp.where(upper, out[:, :, 0], out[:, :, 1])
        theirs = jnp.where(upper, out[:, :, 1], out[:, :, 0]).astype(jnp.bfloat16)
        results.append(mine + lax.ppermute(theirs, "lev", swap).astype(jnp.float32))
    return jnp.concatenate(results[::-1], axis=3)


def solution(mesh):
    nw, nl = mesh.shape["wave"], mesh.shape["lev"]

    def run(spectral, *rest):
        slots, lv = M // nw, spectral.shape[0] // nl
        fits = nl == 2 and NLAT % (nw * nl) == 0 and M % nw == 0 and slots % 8 == 0
        fits = fits and M % LANES == 0 and lv * (NLAT // (nw * nl)) <= LANES and (NLAT // nl) % LANES == 0
        in_specs = (P("lev", None, None, "wave", None), P("wave", "lev", None), P(), P(), P(), P())
        out_specs = P("lev", None, None, "wave", None)
        chosen = body if fits else general_body
        return jax.shard_map(chosen, mesh=mesh, in_specs=in_specs, out_specs=out_specs, check_vma=False)(spectral, *rest)

    return run
```

```python
import math

import jax
import jax.numpy as jnp
from jax import lax
from jax.experimental import pallas as pl
from jax.experimental.pallas import tpu as pltpu
from jax.sharding import PartitionSpec as P

M = 640
NLAT = 1280
NLON = 2560


def wave_tables(wave_list, lon_total):
    lon_ids = jnp.arange(lon_total, dtype=jnp.int32)
    phases = wave_list[:, None] * lon_ids[None, :] % lon_total
    angles = phases.astype(jnp.float32) * (2.0 * math.pi / lon_total)
    cosine = jnp.cos(angles)
    sine_part = jnp.sin(angles)
    weights = jnp.where(wave_list == 0, 1.0, 2.0).astype(jnp.float32)[:, None]
    inverse = jnp.stack([weights * cosine, -(weights * sine_part)], axis=0).astype(jnp.bfloat16)
    factor = 2.0 / lon_total
    direct = jnp.stack([factor * cosine, -(factor * sine_part)], axis=0)
    direct = jnp.transpose(direct, (2, 0, 1)).astype(jnp.bfloat16)
    return (inverse, direct)


def mix_levels(temper, diverg, geopot, omega_vel, sin_lat):
    first_field = geopot + omega_vel * temper
    second_field = sin_lat[None, :, None] * omega_vel + diverg * temper
    return jnp.stack([first_field, second_field], axis=1).astype(jnp.bfloat16)


def general_body(spectral, legendre, thickness, pressure_step, wave_order, lat_order):
    wave_index = lax.axis_index("wave")
    wave_count = lax.axis_size("wave")
    local_slots = legendre.shape[0]
    grid_lats = NLAT // wave_count
    my_waves = lax.dynamic_slice(wave_order, (wave_index * local_slots,), (local_slots,))
    row_ids = jnp.arange(M, dtype=jnp.int32)
    in_triangle = row_ids[None, :] < (M - my_waves)[:, None]
    masked_leg = jnp.where(in_triangle[:, None, :], legendre, jnp.zeros((), jnp.bfloat16))
    fourier = jnp.einsum(
        "lfcsk,sqk->lfcsq",
        lax.all_gather(spectral, "lev", axis=0, tiled=True),
        masked_leg,
        preferred_element_type=jnp.float32,
    ).astype(jnp.bfloat16)
    level_split = lax.all_to_all(fourier, "lev", split_axis=0, concat_axis=4, tiled=True)
    inverse_table, forward_legendre_table = wave_tables(wave_order, NLON)
    grid_vals = jnp.einsum(
        "lfcsq,cst->lfqt",
        lax.all_to_all(level_split, "wave", split_axis=4, concat_axis=3, tiled=True),
        inverse_table,
        preferred_element_type=jnp.float32,
    )
    lat_ids = lax.dynamic_slice(lat_order, (wave_index * grid_lats,), (grid_lats,))
    angles = math.pi * (lat_ids.astype(jnp.float32) + 0.75) / (NLAT + 0.5)
    sin_lat = jnp.cos(angles)
    cos_lat = jnp.sin(angles)
    columns = lax.all_to_all(grid_vals, "lev", split_axis=3, concat_axis=0, tiled=True)
    temper = columns[:, 0]
    diverg = columns[:, 1]
    geopot = jnp.flip(jnp.cumsum(jnp.flip(thickness[:, None, None] * temper, 0), axis=0), 0)
    omega_vel = -jnp.cumsum(pressure_step[:, None, None] * diverg, axis=0)
    tend_cols = mix_levels(temper, diverg, geopot, omega_vel, sin_lat)
    tendency_field = lax.all_to_all(tend_cols, "lev", split_axis=0, concat_axis=3, tiled=True)
    returned_grid_values = (
        jnp.einsum(
            "opgu,ukh->opkhg",
            tendency_field,
            forward_legendre_table,
            preferred_element_type=jnp.float32,
        )
        * cos_lat
    ).astype(jnp.bfloat16)
    band_vals = lax.all_to_all(
        lax.all_to_all(returned_grid_values, "wave", split_axis=3, concat_axis=4, tiled=True),
        "lev",
        split_axis=4,
        concat_axis=0,
        tiled=True,
    )
    summed = lax.psum_scatter(
        jnp.einsum("lfcsq,sqk->lfcsk", band_vals, masked_leg, preferred_element_type=jnp.float32),
        "lev",
        scatter_dimension=0,
        tiled=True,
    )
    return summed


LANES = 128
ROWS = 256
UNROLL = 4
VMEM_LIMIT = 48 * 1024 * 1024


def placed(rows, cols, row_start, col_start, count):
    r = lax.broadcasted_iota(jnp.int32, (rows, cols), 0)
    c = lax.broadcasted_iota(jnp.int32, (rows, cols), 1)
    hit = (r - row_start == c - col_start) & (c >= col_start) & (c < col_start + count)
    return jnp.where(hit, 1.0, 0.0).astype(jnp.bfloat16)


def whole(a):
    return pl.BlockSpec(a.shape, lambda i, n=len(a.shape): (0,) * n)


def greet(nw, wave, lev):
    barrier = pltpu.get_barrier_semaphore()

    @pl.loop(1, nw)
    def _(i):
        pl.semaphore_signal(barrier, inc=1, device_id={"wave": lax.rem(wave + i, nw)}, device_id_type=pl.DeviceIdType.MESH)

    pl.semaphore_signal(barrier, inc=1, device_id={"lev": 1 - lev}, device_id_type=pl.DeviceIdType.MESH)
    pl.semaphore_wait(barrier, nw)


def to_wave(src, dst, slot, target, sends, recvs, i):
    return pltpu.make_async_remote_copy(
        src_ref=src.at[target],
        dst_ref=dst.at[slot],
        send_sem=sends.at[i],
        recv_sem=recvs.at[i],
        device_id={"wave": target},
        device_id_type=pl.DeviceIdType.MESH,
    )


def to_lev(src, dst, lev, send, recv):
    return pltpu.make_async_remote_copy(
        src_ref=src, dst_ref=dst, send_sem=send, recv_sem=recv, device_id={"lev": 1 - lev}, device_id_type=pl.DeviceIdType.MESH
    )


def start_exchange(nw, wave, src, dst, sends, recvs, local):
    @pl.loop(1, nw)
    def _(i):
        to_wave(src, dst, wave, lax.rem(wave + i, nw), sends, recvs, i).start()

    pltpu.make_async_copy(src.at[wave], dst.at[wave], local).start()


def wait_arrivals(nw, wave, src, dst, sends, recvs, local):
    pltpu.make_async_copy(src.at[wave], dst.at[wave], local).wait()

    @pl.loop(1, nw)
    def _(i):
        to_wave(src, dst, lax.rem(wave + nw - i, nw), lax.rem(wave + i, nw), sends, recvs, i).wait_recv()


def wait_sends(nw, wave, src, dst, sends, recvs):
    @pl.loop(1, nw)
    def _(i):
        to_wave(src, dst, wave, lax.rem(wave + i, nw), sends, recvs, i).wait_send()


def inverse_legendre_kernel(groups, slots, lats, lv, nw, *refs):
    count = len(groups)
    owns, refs = refs[:count], refs[count:]
    weight_ref, leg_ref, refs = refs[0], refs[1], refs[2:]
    outs, others, sents, refs = refs[:count], refs[count : 2 * count], refs[2 * count : 3 * count], refs[3 * count :]
    cut, held, lev_send, lev_recv, sends, recvs, local = refs
    step = pl.program_id(0)
    wave, lev = lax.axis_index("wave"), lax.axis_index("lev")
    tiles = cut.shape[0]
    rows = 8 * lv

    @pl.when(step == 0)
    def _():
        greet(nw, wave, lev)
        for g in range(count):
            to_lev(owns[g], others[g], lev, lev_send.at[g], lev_recv.at[g]).start()

    for g, (start, n) in enumerate(groups):

        @pl.when(step == start // UNROLL)
        def _(g=g, start=start, n=n):
            to_lev(owns[g], others[g], lev, lev_send.at[g], lev_recv.at[g]).wait()
            for b in range(tiles):
                lanes = slice(b * LANES, (b + 1) * LANES)
                scale = weight_ref[start : start + n, lanes]
                mine = owns[g][:, lanes].astype(jnp.float32)
                theirs = others[g][:, lanes].astype(jnp.float32)
                for a in range(4 * lv):
                    x, y = mine[a * n : (a + 1) * n] * scale, theirs[a * n : (a + 1) * n] * scale
                    for half in range(2):
                        top = ((a // 2 * 2 + half) * 2 + a % 2) * slots + start
                        cut[b, top : top + n, :] = jnp.where(lev == half, x, y)

    total = None
    for j in range(UNROLL):
        x = jnp.concatenate([cut[b, pl.ds(step * UNROLL + j, rows, stride=slots), :] for b in range(tiles)], axis=1)
        x = jnp.concatenate([x if i == j else jnp.zeros_like(x) for i in range(UNROLL)], axis=0).astype(jnp.bfloat16)
        part = lax.dot_general(leg_ref[j], x, (((1,), (1,)), ((), ())), preferred_element_type=jnp.float32)
        total = part if total is None else total + part
    y = total.T
    blocks = y.shape[1] // LANES
    for j in range(UNROLL):
        for l in range(lv):
            for b in range(blocks):
                r = rows * j + 8 * l
                held[l * blocks + b, pl.ds(step * UNROLL + j, 8, stride=slots), :] = y[r : r + 8, b * LANES : (b + 1) * LANES]

    for g, (start, n) in enumerate(groups):

        @pl.when(step == (start + n) // UNROLL - 1)
        def _(g=g, start=start, n=n):
            packed = [
                jnp.concatenate([held[i, r * slots + start : r * slots + start + n, :] for r in range(8)], axis=0).astype(jnp.bfloat16)
                for i in range(lv * blocks)
            ]
            for d in range(nw):
                total = jnp.zeros((8 * n, LANES), jnp.float32)
                for b in range(lats * d // LANES, (lats * (d + 1) - 1) // LANES + 1):
                    for l in range(lv):
                        first = max(lats * d, LANES * b)
                        last = min(lats * (d + 1), LANES * (b + 1))
                        sel = placed(LANES, LANES, first - LANES * b, lats * l + first - lats * d, last - first)
                        total += jnp.dot(packed[l * blocks + b], sel, preferred_element_type=jnp.float32)
                sents[g][d] = total.astype(jnp.bfloat16)
            start_exchange(nw, wave, sents[g], outs[g], sends.at[g], recvs.at[g], local.at[g])

    @pl.when(step == slots // UNROLL - 1)
    def _():
        for g in range(count):
            wait_arrivals(nw, wave, sents[g], outs[g], sends.at[g], recvs.at[g], local.at[g])
            wait_sends(nw, wave, sents[g], outs[g], sends.at[g], recvs.at[g])


def inverse_legendre(owns, weights, legendre, groups, lv, nw):
    slots, band, rows = legendre.shape
    lats = band // nw
    blocks = [jax.ShapeDtypeStruct((nw, 8 * n, LANES), jnp.bfloat16) for _, n in groups]
    return pl.pallas_call(
        lambda *refs: inverse_legendre_kernel(groups, slots, lats, lv, nw, *refs),
        grid=(slots // UNROLL,),
        in_specs=[whole(a) for a in owns] + [whole(weights), pl.BlockSpec((UNROLL, band, rows), lambda s: (s, 0, 0))],
        out_specs=[pl.BlockSpec(memory_space=pl.ANY)] * len(groups),
        out_shape=blocks,
        scratch_shapes=[pltpu.VMEM(a.shape, a.dtype) for a in owns]
        + [pltpu.VMEM(a.shape, a.dtype) for a in blocks]
        + [
            pltpu.VMEM((rows // LANES, 8 * lv * slots, LANES), jnp.float32),
            pltpu.VMEM((lv * band // LANES, 8 * slots, LANES), jnp.float32),
            pltpu.SemaphoreType.DMA((len(groups),)),
            pltpu.SemaphoreType.DMA((len(groups),)),
            pltpu.SemaphoreType.DMA((len(groups), nw)),
            pltpu.SemaphoreType.DMA((len(groups), nw)),
            pltpu.SemaphoreType.DMA((len(groups),)),
        ],
        compiler_params=pltpu.CompilerParams(vmem_limit_bytes=VMEM_LIMIT, collective_id=0, has_side_effects=True),
        cost_estimate=pl.CostEstimate(flops=2 * slots * band * rows * 256, bytes_accessed=2 * slots * band * rows, transcendentals=0),
        name="inverse_legendre",
    )(*owns, weights, legendre)


def grid_kernel(steps, factor, groups, *refs):
    i = pl.program_id(0)
    recvs, (cos_ref, sin_ref, row_ref, lane_ref, down_ref, up_ref) = refs[:groups], refs[groups : groups + 6]
    outs, (operand, total) = refs[groups + 6 : -2], refs[-2:]

    @pl.when(i == 0)
    def _():
        top = 0
        for recv in recvs:
            nw, half = recv.shape[0], recv.shape[1] // 4
            for j in range(4):
                operand[top : top + nw * half, j * LANES : (j + 1) * LANES] = recv[:, j * half : (j + 1) * half, :].reshape(nw * half, LANES)
            top += nw * half

    parts = []
    for u in range(ROWS // LANES):
        row = row_ref[i * (ROWS // LANES) + u]
        parts.append(cos_ref[...] * row[0:1, :] - sin_ref[...] * row[1:2, :])
    table = jnp.concatenate(parts, axis=0)
    values = jnp.dot(table.astype(jnp.bfloat16), operand[...], preferred_element_type=jnp.float32)
    temper = values[:, : 2 * LANES]
    diverg = values[:, 2 * LANES :]

    def level_sum(x, matrix):
        high = x.astype(jnp.bfloat16)
        low = (x - high.astype(jnp.float32)).astype(jnp.bfloat16)
        return jnp.dot(high, matrix, preferred_element_type=jnp.float32) + jnp.dot(low, matrix, preferred_element_type=jnp.float32)

    geopot = level_sum(temper * lane_ref[0:1, :], up_ref[...])
    omega = -level_sum(diverg * lane_ref[1:2, :], down_ref[...])
    first = geopot + omega * temper
    second = lane_ref[2:3, :] * omega + diverg * temper
    tendency = jnp.concatenate([first, second], axis=1).astype(jnp.bfloat16)
    part = lax.dot_general((table * factor).astype(jnp.bfloat16), tendency, (((0,), (0,)), ((), ())), preferred_element_type=jnp.float32)

    @pl.when(i == 0)
    def _():
        total[...] = part

    @pl.when(i > 0)
    def _():
        total[...] += part

    @pl.when(i == steps - 1)
    def _():
        scale = lane_ref[3:4, :]
        scale = jnp.concatenate([scale, scale], axis=1)
        top = 0
        for out in outs:
            nw, half = out.shape[0], out.shape[1] // 4
            for j in range(4):
                lanes = slice(j * LANES, (j + 1) * LANES)
                block = (total[top : top + nw * half, lanes] * scale[:, lanes]).astype(jnp.bfloat16)
                out[:, j * half : (j + 1) * half, :] = block.reshape(nw, half, LANES)
            top += nw * half


def grid_space(recvs, *tables):
    steps = NLON // ROWS
    waves = tables[0].shape[1]
    args = (*recvs, *tables)
    return pl.pallas_call(
        lambda *refs: grid_kernel(steps, 2.0 / NLON, len(recvs), *refs),
        grid=(steps,),
        in_specs=[whole(a) for a in args],
        out_specs=[whole(a) for a in recvs],
        out_shape=[jax.ShapeDtypeStruct(a.shape, a.dtype) for a in recvs],
        scratch_shapes=[pltpu.VMEM((waves, 4 * LANES), jnp.bfloat16), pltpu.VMEM((waves, 4 * LANES), jnp.float32)],
        compiler_params=pltpu.CompilerParams(vmem_limit_bytes=VMEM_LIMIT),
        cost_estimate=pl.CostEstimate(flops=4 * NLON * waves * 4 * LANES, bytes_accessed=8 * waves * LANES, transcendentals=0),
        name="grid_space",
    )(*args)


def direct_legendre_kernel(order, slots, lats, lv, nw, *refs):
    count = len(order)
    backs, leg_ref, out_ref, refs = refs[:count], refs[count], refs[count + 1], refs[count + 2 :]
    arrived, partials, lands, refs = refs[:count], refs[count : 2 * count], refs[2 * count : 3 * count], refs[3 * count :]
    held, cut, lev_send, lev_recv, sends, recvs, local = refs
    step = pl.program_id(0)
    wave, lev = lax.axis_index("wave"), lax.axis_index("lev")
    blocks = leg_ref.shape[1] // LANES
    tiles = cut.shape[0]
    base = order[0][0]

    @pl.when(step == 0)
    def _():
        greet(nw, wave, lev)
        for g in range(count):
            start_exchange(nw, wave, backs[g], arrived[g], sends.at[g], recvs.at[g], local.at[g])

    for g, (start, n) in enumerate(order):

        @pl.when(step == (start - base) % slots // UNROLL)
        def _(g=g, start=start, n=n):
            wait_arrivals(nw, wave, backs[g], arrived[g], sends.at[g], recvs.at[g], local.at[g])
            for b in range(blocks):
                total = jnp.zeros((8 * n, lv * LANES), jnp.float32)
                for w in range(LANES * b // lats, (LANES * (b + 1) - 1) // lats + 1):
                    first = max(lats * w, LANES * b)
                    last = min(lats * (w + 1), LANES * (b + 1))
                    sel = jnp.concatenate(
                        [placed(LANES, LANES, lats * l + first - lats * w, first - LANES * b, last - first) for l in range(lv)], axis=1
                    )
                    total += jnp.dot(arrived[g][w], sel, preferred_element_type=jnp.float32)
                for l in range(lv):
                    for r in range(8):
                        top = r * slots + start
                        held[l * blocks + b, top : top + n, :] = total[r * n : (r + 1) * n, l * LANES : (l + 1) * LANES]

    for j in range(UNROLL):
        s = lax.rem(step * UNROLL + base, slots) + j
        x = jnp.concatenate(
            [jnp.concatenate([held[l * blocks + b, pl.ds(s, 8, stride=slots), :] for b in range(blocks)], axis=1) for l in range(lv)], axis=0
        ).astype(jnp.bfloat16)
        y = jnp.dot(x, leg_ref[j], preferred_element_type=jnp.float32)
        for b in range(tiles):
            cut[b, pl.ds(s, 8 * lv, stride=slots), :] = y[:, b * LANES : (b + 1) * LANES]

    def halves(b, start, n):
        found = ([], [])
        for a in range(4 * lv):
            x, y = [cut[b, pl.ds(((a // 2 * 2 + half) * 2 + a % 2) * slots + start, n), :] for half in range(2)]
            found[0].append(jnp.where(lev == 0, x, y))
            found[1].append(jnp.where(lev == 0, y, x))
        return found

    for g, (start, n) in enumerate(order):

        @pl.when(step == ((start - base) % slots + n) // UNROLL - 1)
        def _(g=g, start=start, n=n):
            for b in range(tiles):
                theirs = halves(b, start, n)[1]
                partials[g][:, b * LANES : (b + 1) * LANES] = jnp.concatenate(theirs, axis=0).astype(jnp.bfloat16)
            to_lev(partials[g], lands[g], lev, lev_send.at[g], lev_recv.at[g]).start()

    @pl.when(step == slots // UNROLL - 1)
    def _():
        for g, (start, n) in enumerate(order):
            wait_sends(nw, wave, backs[g], arrived[g], sends.at[g], recvs.at[g])
        for g, (start, n) in enumerate(order):
            to_lev(partials[g], lands[g], lev, lev_send.at[g], lev_recv.at[g]).wait()
            for b in range(tiles):
                lanes = slice(b * LANES, (b + 1) * LANES)
                mine = halves(b, start, n)[0]
                land = lands[g][:, lanes].astype(jnp.float32)
                for a in range(4 * lv):
                    out_ref[a * slots + start : a * slots + start + n, lanes] = mine[a] + land[a * n : (a + 1) * n]


def direct_legendre(backs, legendre, order, lv):
    slots, band, rows = legendre.shape
    nw = backs[0].shape[0]
    lats = band // nw
    base = order[0][0] // UNROLL
    shares = [pltpu.VMEM((4 * lv * n, rows), jnp.bfloat16) for _, n in order]
    return pl.pallas_call(
        lambda *refs: direct_legendre_kernel(order, slots, lats, lv, nw, *refs),
        grid=(slots // UNROLL,),
        in_specs=[pl.BlockSpec(memory_space=pl.ANY)] * len(order)
        + [pl.BlockSpec((UNROLL, band, rows), lambda s: (lax.rem(s + base, slots // UNROLL), 0, 0))],
        out_specs=pl.BlockSpec((4 * lv * slots, rows), lambda s: (0, 0)),
        out_shape=jax.ShapeDtypeStruct((4 * lv * slots, rows), jnp.float32),
        scratch_shapes=[pltpu.VMEM(a.shape, a.dtype) for a in backs]
        + shares
        + shares
        + [
            pltpu.VMEM((lv * band // LANES, 8 * slots, LANES), jnp.float32),
            pltpu.VMEM((rows // LANES, 8 * lv * slots, LANES), jnp.float32),
            pltpu.SemaphoreType.DMA((len(order),)),
            pltpu.SemaphoreType.DMA((len(order),)),
            pltpu.SemaphoreType.DMA((len(order), nw)),
            pltpu.SemaphoreType.DMA((len(order), nw)),
            pltpu.SemaphoreType.DMA((len(order),)),
        ],
        compiler_params=pltpu.CompilerParams(vmem_limit_bytes=VMEM_LIMIT, collective_id=1, has_side_effects=True),
        cost_estimate=pl.CostEstimate(flops=2 * slots * band * rows * 256, bytes_accessed=2 * slots * band * rows, transcendentals=0),
        name="direct_legendre",
    )(*backs, legendre)


def body(spectral, legendre, thickness, pressure_step, wave_order, lat_order):
    wave_index = lax.axis_index("wave")
    lev_index = lax.axis_index("lev")
    nw = lax.axis_size("wave")
    slots, band, rows = legendre.shape
    lats = band // nw
    lv = spectral.shape[0]
    cutoff = slots * 2 // 5 // 8 * 8
    groups = [(0, cutoff), (cutoff, slots - cutoff)] if cutoff else [(0, slots)]
    owns = [spectral[:, :, :, start : start + n].reshape(4 * lv * n, rows) for start, n in groups]
    my_waves = lax.dynamic_slice(wave_order, (wave_index * slots,), (slots,))
    in_triangle = jnp.arange(rows, dtype=jnp.int32)[None, :] < (M - my_waves)[:, None]
    weights = jnp.where(my_waves == 0, 1.0, 2.0).astype(jnp.float32)[:, None]
    weights = jnp.where(in_triangle, weights, 0.0)

    by_device = wave_order.reshape(nw, 1, slots)
    lane_waves = jnp.concatenate(
        [jnp.broadcast_to(by_device[:, :, start : start + n], (nw, 2, n)).reshape(1, -1) for start, n in groups], axis=1
    )
    imaginary = jnp.concatenate([jnp.arange(2 * nw * n) // n % 2 == 1 for _, n in groups])[None, :]
    turn = 2.0 * math.pi / NLON
    inner = (lane_waves * jnp.arange(LANES, dtype=jnp.int32)[:, None] % NLON).astype(jnp.float32) * turn
    cos_base, sin_base = jnp.cos(inner), jnp.sin(inner)
    outer = (lane_waves * jnp.arange(0, NLON, LANES, dtype=jnp.int32)[:, None] % NLON).astype(jnp.float32) * turn
    cos_outer, sin_outer = jnp.cos(outer), jnp.sin(outer)
    row_table = jnp.stack([jnp.where(imaginary, -sin_outer, cos_outer), jnp.where(imaginary, cos_outer, sin_outer)], axis=1)

    lat_ids = lax.dynamic_slice(lat_order, (lev_index * band + wave_index * lats,), (lats,))
    angles = math.pi * (lat_ids.astype(jnp.float32) + 0.75) / (NLAT + 0.5)

    def lanes(by_level_lat):
        pad = LANES - lv * lats
        return jnp.pad(by_level_lat.reshape(2, lv * lats), ((0, 0), (0, pad))).reshape(2 * LANES)

    spread = jnp.ones((2 * lv, lats), jnp.float32)
    zero = jnp.zeros((2 * LANES,), jnp.float32)
    lane_values = jnp.stack(
        [lanes(thickness[:, None] * spread), lanes(pressure_step[:, None] * spread), lanes(jnp.cos(angles) * spread), lanes(jnp.sin(angles) * spread)]
        + [zero] * 4
    )
    place = jnp.arange(2 * LANES)
    valid = place % LANES < lv * lats
    level = place // LANES * lv + place % LANES // lats
    lat = place % LANES % lats
    same = (lat[:, None] == lat[None, :]) & valid[:, None] & valid[None, :]
    down = (same & (level[:, None] <= level[None, :])).astype(jnp.bfloat16)
    up = (same & (level[:, None] >= level[None, :])).astype(jnp.bfloat16)

    recvs = inverse_legendre(owns, weights, legendre, groups, lv, nw)
    backs = grid_space(recvs, cos_base, sin_base, row_table, lane_values, down, up)
    out = direct_legendre(backs[::-1], legendre, groups[::-1], lv).reshape(lv, 2, 2, slots, rows)
    return jnp.where(in_triangle, out, 0.0)


def solution(mesh):
    nw, nl = mesh.shape["wave"], mesh.shape["lev"]

    def run(spectral, *rest):
        slots, lv = M // nw, spectral.shape[0] // nl
        fits = nl == 2 and NLAT % (nw * nl) == 0 and M % nw == 0 and slots % 8 == 0
        fits = fits and M % LANES == 0 and lv * (NLAT // (nw * nl)) <= LANES and (NLAT // nl) % LANES == 0
        in_specs = (P("lev", None, None, "wave", None), P("wave", "lev", None), P(), P(), P(), P())
        out_specs = P("lev", None, None, "wave", None)
        chosen = body if fits else general_body
        return jax.shard_map(chosen, mesh=mesh, in_specs=in_specs, out_specs=out_specs, check_vma=False)(spectral, *rest)

    return run
```

```python
import math

import jax
import jax.numpy as jnp
from jax import lax
from jax.experimental import pallas as pl
from jax.experimental.pallas import tpu as pltpu
from jax.sharding import PartitionSpec as P

M = 640
NLAT = 1280
NLON = 2560


def wave_tables(wave_list, lon_total):
    lon_ids = jnp.arange(lon_total, dtype=jnp.int32)
    phases = wave_list[:, None] * lon_ids[None, :] % lon_total
    angles = phases.astype(jnp.float32) * (2.0 * math.pi / lon_total)
    cosine = jnp.cos(angles)
    sine_part = jnp.sin(angles)
    weights = jnp.where(wave_list == 0, 1.0, 2.0).astype(jnp.float32)[:, None]
    inverse = jnp.stack([weights * cosine, -(weights * sine_part)], axis=0).astype(jnp.bfloat16)
    factor = 2.0 / lon_total
    direct = jnp.stack([factor * cosine, -(factor * sine_part)], axis=0)
    direct = jnp.transpose(direct, (2, 0, 1)).astype(jnp.bfloat16)
    return (inverse, direct)


def mix_levels(temper, diverg, geopot, omega_vel, sin_lat):
    first_field = geopot + omega_vel * temper
    second_field = sin_lat[None, :, None] * omega_vel + diverg * temper
    return jnp.stack([first_field, second_field], axis=1).astype(jnp.bfloat16)


def general_body(spectral, legendre, thickness, pressure_step, wave_order, lat_order):
    wave_index = lax.axis_index("wave")
    wave_count = lax.axis_size("wave")
    local_slots = legendre.shape[0]
    grid_lats = NLAT // wave_count
    my_waves = lax.dynamic_slice(wave_order, (wave_index * local_slots,), (local_slots,))
    row_ids = jnp.arange(M, dtype=jnp.int32)
    in_triangle = row_ids[None, :] < (M - my_waves)[:, None]
    masked_leg = jnp.where(in_triangle[:, None, :], legendre, jnp.zeros((), jnp.bfloat16))
    fourier = jnp.einsum(
        "lfcsk,sqk->lfcsq",
        lax.all_gather(spectral, "lev", axis=0, tiled=True),
        masked_leg,
        preferred_element_type=jnp.float32,
    ).astype(jnp.bfloat16)
    level_split = lax.all_to_all(fourier, "lev", split_axis=0, concat_axis=4, tiled=True)
    inverse_table, forward_legendre_table = wave_tables(wave_order, NLON)
    grid_vals = jnp.einsum(
        "lfcsq,cst->lfqt",
        lax.all_to_all(level_split, "wave", split_axis=4, concat_axis=3, tiled=True),
        inverse_table,
        preferred_element_type=jnp.float32,
    )
    lat_ids = lax.dynamic_slice(lat_order, (wave_index * grid_lats,), (grid_lats,))
    angles = math.pi * (lat_ids.astype(jnp.float32) + 0.75) / (NLAT + 0.5)
    sin_lat = jnp.cos(angles)
    cos_lat = jnp.sin(angles)
    columns = lax.all_to_all(grid_vals, "lev", split_axis=3, concat_axis=0, tiled=True)
    temper = columns[:, 0]
    diverg = columns[:, 1]
    geopot = jnp.flip(jnp.cumsum(jnp.flip(thickness[:, None, None] * temper, 0), axis=0), 0)
    omega_vel = -jnp.cumsum(pressure_step[:, None, None] * diverg, axis=0)
    tend_cols = mix_levels(temper, diverg, geopot, omega_vel, sin_lat)
    tendency_field = lax.all_to_all(tend_cols, "lev", split_axis=0, concat_axis=3, tiled=True)
    returned_grid_values = (
        jnp.einsum(
            "opgu,ukh->opkhg",
            tendency_field,
            forward_legendre_table,
            preferred_element_type=jnp.float32,
        )
        * cos_lat
    ).astype(jnp.bfloat16)
    band_vals = lax.all_to_all(
        lax.all_to_all(returned_grid_values, "wave", split_axis=3, concat_axis=4, tiled=True),
        "lev",
        split_axis=4,
        concat_axis=0,
        tiled=True,
    )
    summed = lax.psum_scatter(
        jnp.einsum("lfcsq,sqk->lfcsk", band_vals, masked_leg, preferred_element_type=jnp.float32),
        "lev",
        scatter_dimension=0,
        tiled=True,
    )
    return summed


LANES = 128
ROWS = 640
GROUP = 8
UNROLL = 4
VMEM_LIMIT = 48 * 1024 * 1024


def placed(rows, cols, row_start, col_start, count):
    r = lax.broadcasted_iota(jnp.int32, (rows, cols), 0)
    c = lax.broadcasted_iota(jnp.int32, (rows, cols), 1)
    hit = (r - row_start == c - col_start) & (c >= col_start) & (c < col_start + count)
    return jnp.where(hit, 1.0, 0.0).astype(jnp.bfloat16)


def whole(a):
    return pl.BlockSpec(a.shape, lambda i, n=len(a.shape): (0,) * n)


def greet(nw, wave, lev):
    barrier = pltpu.get_barrier_semaphore()

    @pl.loop(1, nw)
    def _(i):
        pl.semaphore_signal(barrier, inc=1, device_id={"wave": lax.rem(wave + i, nw)}, device_id_type=pl.DeviceIdType.MESH)

    pl.semaphore_signal(barrier, inc=1, device_id={"lev": 1 - lev}, device_id_type=pl.DeviceIdType.MESH)
    pl.semaphore_wait(barrier, nw)


def to_wave(src, dst, slot, target, sends, recvs, i):
    return pltpu.make_async_remote_copy(
        src_ref=src.at[target],
        dst_ref=dst.at[slot],
        send_sem=sends.at[i],
        recv_sem=recvs.at[i],
        device_id={"wave": target},
        device_id_type=pl.DeviceIdType.MESH,
    )


def to_lev(src, dst, lev, send, recv):
    return pltpu.make_async_remote_copy(
        src_ref=src, dst_ref=dst, send_sem=send, recv_sem=recv, device_id={"lev": 1 - lev}, device_id_type=pl.DeviceIdType.MESH
    )


def start_exchange(nw, wave, src, dst, sends, recvs, local):
    @pl.loop(1, nw)
    def _(i):
        to_wave(src, dst, wave, lax.rem(wave + i, nw), sends, recvs, i).start()

    pltpu.make_async_copy(src.at[wave], dst.at[wave], local).start()


def wait_arrivals(nw, wave, src, dst, sends, recvs, local):
    pltpu.make_async_copy(src.at[wave], dst.at[wave], local).wait()

    @pl.loop(1, nw)
    def _(i):
        to_wave(src, dst, lax.rem(wave + nw - i, nw), lax.rem(wave + i, nw), sends, recvs, i).wait_recv()


def wait_sends(nw, wave, src, dst, sends, recvs):
    @pl.loop(1, nw)
    def _(i):
        to_wave(src, dst, wave, lax.rem(wave + i, nw), sends, recvs, i).wait_send()


def fill_tables(waves, cos_ref, sin_ref, row_ref):
    turn = 2.0 * math.pi / NLON

    def angle(times):
        phase = waves * times
        return (phase - NLON * jnp.floor((phase + 0.5) * (1.0 / NLON))) * turn

    inner = angle(lax.broadcasted_iota(jnp.int32, cos_ref.shape, 0).astype(jnp.float32))
    cos_ref[...] = jnp.cos(inner)
    sin_ref[...] = jnp.sin(inner)
    blocks = row_ref.shape[1]
    outer = angle(lax.broadcasted_iota(jnp.int32, row_ref.shape[1:], 0).astype(jnp.float32) * float(LANES))
    cosine, sine = jnp.cos(outer), jnp.sin(outer)
    imaginary = lax.broadcasted_iota(jnp.int32, cosine.shape, 1) // GROUP % 2 == 1
    row_ref[0] = jnp.where(imaginary, -sine, cosine)
    row_ref[1] = jnp.where(imaginary, cosine, sine)


def inverse_legendre_kernel(slots, lats, lv, nw, *refs):
    wave_ref, lane_wave_ref, own, leg_ref, out, cos_ref, sin_ref, row_ref = refs[:8]
    other, sent, cut, held, lev_send, lev_recv, sends, recvs, local = refs[8:]
    step = pl.program_id(0)
    wave, lev = lax.axis_index("wave"), lax.axis_index("lev")
    tiles = cut.shape[0]
    rows = 8 * lv
    n = GROUP
    count = slots // n
    per_group = n // UNROLL

    @pl.when(step == 0)
    def _():
        greet(nw, wave, lev)
        for g in range(count):
            to_lev(own.at[g], other.at[g], lev, lev_send.at[g], lev_recv.at[g]).start()

    @pl.when(lax.rem(step, per_group) == 0)
    def _():
        g = step // per_group
        to_lev(own.at[g], other.at[g], lev, lev_send.at[g], lev_recv.at[g]).wait()
        for b in range(tiles):
            lanes = slice(b * LANES, (b + 1) * LANES)
            mine = own[g, :, lanes].astype(jnp.float32)
            theirs = other[g, :, lanes].astype(jnp.float32)
            for a in range(4 * lv):
                x, y = mine[a * n : (a + 1) * n], theirs[a * n : (a + 1) * n]
                for half in range(2):
                    top = ((a // 2 * 2 + half) * 2 + a % 2) * n
                    cut[b, top : top + n, :] = jnp.where(lev == half, x, y)

    total = None
    for j in range(UNROLL):
        s = lax.rem(step, per_group) * UNROLL + j
        m = wave_ref[wave * slots + step * UNROLL + j]
        x = jnp.concatenate([cut[b, pl.ds(s, rows, stride=n), :] for b in range(tiles)], axis=1)
        k = lax.broadcasted_iota(jnp.int32, x.shape, 1)
        x = jnp.where(k < M - m, x * jnp.where(m == 0, 1.0, 2.0), 0.0)
        x = jnp.concatenate([x if i == j else jnp.zeros_like(x) for i in range(UNROLL)], axis=0).astype(jnp.bfloat16)
        part = lax.dot_general(leg_ref[j], x, (((1,), (1,)), ((), ())), preferred_element_type=jnp.float32)
        total = part if total is None else total + part
    y = total.T
    blocks = y.shape[1] // LANES
    for j in range(UNROLL):
        s = lax.rem(step, per_group) * UNROLL + j
        for l in range(lv):
            for b in range(blocks):
                r = rows * j + 8 * l
                held[l * blocks + b, pl.ds(s, 8, stride=n), :] = y[r : r + 8, b * LANES : (b + 1) * LANES]

    @pl.when(lax.rem(step, per_group) == per_group - 1)
    def _():
        g = step // per_group
        packed = [held[i].astype(jnp.bfloat16) for i in range(lv * blocks)]
        for d in range(nw):
            total = jnp.zeros((8 * n, LANES), jnp.float32)
            for b in range(lats * d // LANES, (lats * (d + 1) - 1) // LANES + 1):
                for l in range(lv):
                    first = max(lats * d, LANES * b)
                    last = min(lats * (d + 1), LANES * (b + 1))
                    sel = placed(LANES, LANES, first - LANES * b, lats * l + first - lats * d, last - first)
                    total += jnp.dot(packed[l * blocks + b], sel, preferred_element_type=jnp.float32)
            sent[g, d] = total.astype(jnp.bfloat16)
        start_exchange(nw, wave, sent.at[g], out.at[g], sends.at[g], recvs.at[g], local.at[g])

    @pl.when(step == slots // UNROLL - 1)
    def _():
        fill_tables(lane_wave_ref[...], cos_ref, sin_ref, row_ref)

        @pl.loop(0, count)
        def _(g):
            wait_arrivals(nw, wave, sent.at[g], out.at[g], sends.at[g], recvs.at[g], local.at[g])
            wait_sends(nw, wave, sent.at[g], out.at[g], sends.at[g], recvs.at[g])


def inverse_legendre(wave_order, lane_waves, own, legendre, lv, nw):
    slots, band, rows = legendre.shape
    lats = band // nw
    count = slots // GROUP
    waves = lane_waves.shape[1]
    block = jax.ShapeDtypeStruct((count, nw, 8 * GROUP, LANES), jnp.bfloat16)
    base = jax.ShapeDtypeStruct((LANES, waves), jnp.float32)
    row = jax.ShapeDtypeStruct((2, NLON // 2 // LANES, waves), jnp.float32)
    return pl.pallas_call(
        lambda *refs: inverse_legendre_kernel(slots, lats, lv, nw, *refs),
        grid=(slots // UNROLL,),
        in_specs=[
            pl.BlockSpec(memory_space=pltpu.SMEM),
            whole(lane_waves),
            whole(own),
            pl.BlockSpec((UNROLL, band, rows), lambda s: (s, 0, 0)),
        ],
        out_specs=[pl.BlockSpec(memory_space=pl.ANY), whole(base), whole(base), whole(row)],
        out_shape=[block, base, base, row],
        scratch_shapes=[
            pltpu.VMEM(own.shape, own.dtype),
            pltpu.VMEM(block.shape, block.dtype),
            pltpu.VMEM((rows // LANES, 8 * lv * GROUP, LANES), jnp.float32),
            pltpu.VMEM((lv * band // LANES, 8 * GROUP, LANES), jnp.float32),
            pltpu.SemaphoreType.DMA((count,)),
            pltpu.SemaphoreType.DMA((count,)),
            pltpu.SemaphoreType.DMA((count, nw)),
            pltpu.SemaphoreType.DMA((count, nw)),
            pltpu.SemaphoreType.DMA((count,)),
        ],
        compiler_params=pltpu.CompilerParams(vmem_limit_bytes=VMEM_LIMIT, collective_id=0, has_side_effects=True),
        cost_estimate=pl.CostEstimate(flops=2 * slots * band * rows * 256, bytes_accessed=2 * slots * band * rows, transcendentals=0),
        name="inverse_legendre",
    )(wave_order, lane_waves, own, legendre)


def grid_kernel(steps, factor, recv, cos_ref, sin_ref, row_ref, lane_ref, sign_ref, down_ref, up_ref, out, operand, total, signs):
    i = pl.program_id(0)
    half = recv.shape[2] // 4
    waves = operand.shape[0]

    @pl.when(i == 0)
    def _():
        signs[...] = jnp.broadcast_to(sign_ref[...], (LANES, waves)).T
        for j in range(4):
            block = recv[:, :, j * half : (j + 1) * half, :].reshape(waves, LANES)
            operand[:, j * LANES : (j + 1) * LANES] = block
            operand[:, (4 + j) * LANES : (5 + j) * LANES] = (block.astype(jnp.float32) * signs[...]).astype(jnp.bfloat16)

    parts = []
    for u in range(ROWS // LANES):
        at = i * (ROWS // LANES) + u
        parts.append(cos_ref[...] * row_ref[0, pl.ds(at, 1), :] - sin_ref[...] * row_ref[1, pl.ds(at, 1), :])
    table = jnp.concatenate(parts, axis=0)

    def level_sum(x, matrix):
        high = x.astype(jnp.bfloat16)
        low = (x - high.astype(jnp.float32)).astype(jnp.bfloat16)
        return jnp.dot(high, matrix, preferred_element_type=jnp.float32) + jnp.dot(low, matrix, preferred_element_type=jnp.float32)

    values = jnp.dot(table.astype(jnp.bfloat16), operand[...], preferred_element_type=jnp.float32)
    tendency = []
    for side in range(2):
        temper = values[:, 4 * LANES * side : 4 * LANES * side + 2 * LANES]
        diverg = values[:, 4 * LANES * side + 2 * LANES : 4 * LANES * (side + 1)]
        geopot = level_sum(temper * lane_ref[0:1, :], up_ref[...])
        omega = -level_sum(diverg * lane_ref[1:2, :], down_ref[...])
        tendency.append((geopot + omega * temper).astype(jnp.bfloat16))
        tendency.append((lane_ref[2:3, :] * omega + diverg * temper).astype(jnp.bfloat16))
    tendency = jnp.concatenate(tendency, axis=1)
    part = lax.dot_general((table * factor).astype(jnp.bfloat16), tendency, (((0,), (0,)), ((), ())), preferred_element_type=jnp.float32)

    @pl.when(i == 0)
    def _():
        total[...] = part

    @pl.when(i > 0)
    def _():
        total[...] += part

    @pl.when(i == steps - 1)
    def _():
        for j in range(4):
            scale = lane_ref[3:4, j % 2 * LANES : (j % 2 + 1) * LANES]
            block = total[:, j * LANES : (j + 1) * LANES] + signs[...] * total[:, (4 + j) * LANES : (5 + j) * LANES]
            block = (block * scale).astype(jnp.bfloat16)
            out[:, :, j * half : (j + 1) * half, :] = block.reshape(recv.shape[0], recv.shape[1], half, LANES)


def grid_space(*args):
    steps = NLON // 2 // ROWS
    waves = args[1].shape[1]
    recv = args[0]
    return pl.pallas_call(
        lambda *refs: grid_kernel(steps, 2.0 / NLON, *refs),
        grid=(steps,),
        in_specs=[whole(a) for a in args],
        out_specs=whole(recv),
        out_shape=jax.ShapeDtypeStruct(recv.shape, recv.dtype),
        scratch_shapes=[
            pltpu.VMEM((waves, 8 * LANES), jnp.bfloat16),
            pltpu.VMEM((waves, 8 * LANES), jnp.float32),
            pltpu.VMEM((waves, LANES), jnp.float32),
        ],
        compiler_params=pltpu.CompilerParams(vmem_limit_bytes=VMEM_LIMIT),
        cost_estimate=pl.CostEstimate(flops=4 * NLON * waves * 4 * LANES, bytes_accessed=8 * waves * LANES, transcendentals=0),
        name="grid_space",
    )(*args)


def direct_legendre_kernel(slots, lats, lv, nw, *refs):
    wave_ref, back, leg_ref, out_ref, arrived, partial, land, held, cut, lev_send, lev_recv, sends, recvs, local = refs
    step = pl.program_id(0)
    wave, lev = lax.axis_index("wave"), lax.axis_index("lev")
    blocks = leg_ref.shape[1] // LANES
    tiles = cut.shape[0]
    n = GROUP
    count = slots // n
    per_group = n // UNROLL

    @pl.when(step == 0)
    def _():
        greet(nw, wave, lev)

        @pl.loop(0, count)
        def _(g):
            start_exchange(nw, wave, back.at[g], arrived.at[g], sends.at[g], recvs.at[g], local.at[g])

    @pl.when(lax.rem(step, per_group) == 0)
    def _():
        g = step // per_group
        wait_arrivals(nw, wave, back.at[g], arrived.at[g], sends.at[g], recvs.at[g], local.at[g])
        for b in range(blocks):
            total = jnp.zeros((8 * n, lv * LANES), jnp.float32)
            for w in range(LANES * b // lats, (LANES * (b + 1) - 1) // lats + 1):
                first = max(lats * w, LANES * b)
                last = min(lats * (w + 1), LANES * (b + 1))
                sel = jnp.concatenate(
                    [placed(LANES, LANES, lats * l + first - lats * w, first - LANES * b, last - first) for l in range(lv)], axis=1
                )
                total += jnp.dot(arrived[g, w], sel, preferred_element_type=jnp.float32)
            for l in range(lv):
                held[l * blocks + b] = total[:, l * LANES : (l + 1) * LANES]

    for j in range(UNROLL):
        s = lax.rem(step, per_group) * UNROLL + j
        x = jnp.concatenate(
            [jnp.concatenate([held[l * blocks + b, pl.ds(s, 8, stride=n), :] for b in range(blocks)], axis=1) for l in range(lv)], axis=0
        ).astype(jnp.bfloat16)
        y = jnp.dot(x, leg_ref[j], preferred_element_type=jnp.float32)
        k = lax.broadcasted_iota(jnp.int32, y.shape, 1)
        y = jnp.where(k < M - wave_ref[wave * slots + step * UNROLL + j], y, 0.0)
        for b in range(tiles):
            cut[b, pl.ds(s, 8 * lv, stride=n), :] = y[:, b * LANES : (b + 1) * LANES]

    @pl.when(lax.rem(step, per_group) == per_group - 1)
    def _():
        g = step // per_group
        start = pl.multiple_of(g * n, n)
        for b in range(tiles):
            lanes = slice(b * LANES, (b + 1) * LANES)
            theirs = []
            for a in range(4 * lv):
                x, y = [cut[b, pl.ds(((a // 2 * 2 + half) * 2 + a % 2) * n, n), :] for half in range(2)]
                theirs.append(jnp.where(lev == 0, y, x))
                out_ref[pl.ds(a * slots + start, n), lanes] = jnp.where(lev == 0, x, y)
            partial[g, :, lanes] = jnp.concatenate(theirs, axis=0).astype(jnp.bfloat16)
        to_lev(partial.at[g], land.at[g], lev, lev_send.at[g], lev_recv.at[g]).start()

    @pl.when(step == slots // UNROLL - 1)
    def _():
        @pl.loop(0, count)
        def _(g):
            wait_sends(nw, wave, back.at[g], arrived.at[g], sends.at[g], recvs.at[g])

        for g in range(count):
            to_lev(partial.at[g], land.at[g], lev, lev_send.at[g], lev_recv.at[g]).wait()
            for b in range(tiles):
                lanes = slice(b * LANES, (b + 1) * LANES)
                theirs = land[g, :, lanes].astype(jnp.float32)
                for a in range(4 * lv):
                    out_ref[a * slots + g * n : a * slots + (g + 1) * n, lanes] += theirs[a * n : (a + 1) * n]


def direct_legendre(wave_order, back, legendre, lv):
    slots, band, rows = legendre.shape
    nw = back.shape[1]
    lats = band // nw
    count = slots // GROUP
    share = pltpu.VMEM((count, 4 * lv * GROUP, rows), jnp.bfloat16)
    return pl.pallas_call(
        lambda *refs: direct_legendre_kernel(slots, lats, lv, nw, *refs),
        grid=(slots // UNROLL,),
        in_specs=[
            pl.BlockSpec(memory_space=pltpu.SMEM),
            pl.BlockSpec(memory_space=pl.ANY),
            pl.BlockSpec((UNROLL, band, rows), lambda s: (s, 0, 0)),
        ],
        out_specs=pl.BlockSpec((4 * lv * slots, rows), lambda s: (0, 0)),
        out_shape=jax.ShapeDtypeStruct((4 * lv * slots, rows), jnp.float32),
        scratch_shapes=[
            pltpu.VMEM(back.shape, back.dtype),
            share,
            share,
            pltpu.VMEM((lv * band // LANES, 8 * GROUP, LANES), jnp.float32),
            pltpu.VMEM((rows // LANES, 8 * lv * GROUP, LANES), jnp.float32),
            pltpu.SemaphoreType.DMA((count,)),
            pltpu.SemaphoreType.DMA((count,)),
            pltpu.SemaphoreType.DMA((count, nw)),
            pltpu.SemaphoreType.DMA((count, nw)),
            pltpu.SemaphoreType.DMA((count,)),
        ],
        compiler_params=pltpu.CompilerParams(vmem_limit_bytes=VMEM_LIMIT, collective_id=1, has_side_effects=True),
        cost_estimate=pl.CostEstimate(flops=2 * slots * band * rows * 256, bytes_accessed=2 * slots * band * rows, transcendentals=0),
        name="direct_legendre",
    )(wave_order, back, legendre)


def body(spectral, legendre, thickness, pressure_step, wave_order, lat_order):
    wave_index = lax.axis_index("wave")
    lev_index = lax.axis_index("lev")
    nw = lax.axis_size("wave")
    slots, band, rows = legendre.shape
    lats = band // nw
    lv = spectral.shape[0]
    count = slots // GROUP
    own = spectral.reshape(4 * lv, count, GROUP, rows).swapaxes(0, 1).reshape(count, 4 * lv * GROUP, rows)
    by_group = wave_order.reshape(nw, count, 1, GROUP).swapaxes(0, 1)
    lane_waves = jnp.broadcast_to(by_group, (count, nw, 2, GROUP)).reshape(1, -1)
    signs = (1 - 2 * (lane_waves % 2)).astype(jnp.float32)
    lane_waves = lane_waves.astype(jnp.float32)

    lat_ids = lax.dynamic_slice(lat_order, (lev_index * band + wave_index * lats,), (lats,))
    angles = math.pi * (lat_ids.astype(jnp.float32) + 0.75) / (NLAT + 0.5)

    def lanes(by_level_lat):
        pad = LANES - lv * lats
        return jnp.pad(by_level_lat.reshape(2, lv * lats), ((0, 0), (0, pad))).reshape(2 * LANES)

    spread = jnp.ones((2 * lv, lats), jnp.float32)
    zero = jnp.zeros((2 * LANES,), jnp.float32)
    lane_values = jnp.stack(
        [lanes(thickness[:, None] * spread), lanes(pressure_step[:, None] * spread), lanes(jnp.cos(angles) * spread), lanes(jnp.sin(angles) * spread)]
        + [zero] * 4
    )
    place = jnp.arange(2 * LANES)
    valid = place % LANES < lv * lats
    level = place // LANES * lv + place % LANES // lats
    lat = place % LANES % lats
    same = (lat[:, None] == lat[None, :]) & valid[:, None] & valid[None, :]
    down = (same & (level[:, None] <= level[None, :])).astype(jnp.bfloat16)
    up = (same & (level[:, None] >= level[None, :])).astype(jnp.bfloat16)

    recv, cos_base, sin_base, row_table = inverse_legendre(wave_order, lane_waves, own, legendre, lv, nw)
    back = grid_space(recv, cos_base, sin_base, row_table, lane_values, signs, down, up)
    out = direct_legendre(wave_order, back, legendre, lv)
    return out.reshape(lv, 2, 2, slots, rows)


def solution(mesh):
    nw, nl = mesh.shape["wave"], mesh.shape["lev"]

    def run(spectral, *rest):
        slots, lv = M // nw, spectral.shape[0] // nl
        fits = nl == 2 and NLAT % (nw * nl) == 0 and M % nw == 0 and slots % GROUP == 0
        fits = fits and M % LANES == 0 and lv * (NLAT // (nw * nl)) <= LANES and (NLAT // nl) % LANES == 0
        in_specs = (P("lev", None, None, "wave", None), P("wave", "lev", None), P(), P(), P(), P())
        out_specs = P("lev", None, None, "wave", None)
        chosen = body if fits else general_body
        return jax.shard_map(chosen, mesh=mesh, in_specs=in_specs, out_specs=out_specs, check_vma=False)(spectral, *rest)

    return run
```

```python
import math

import jax
import jax.numpy as jnp
from jax import lax
from jax.experimental import pallas as pl
from jax.experimental.pallas import tpu as pltpu
from jax.sharding import PartitionSpec as P

M = 640
NLAT = 1280
NLON = 2560


def wave_tables(wave_list, lon_total):
    lon_ids = jnp.arange(lon_total, dtype=jnp.int32)
    phases = wave_list[:, None] * lon_ids[None, :] % lon_total
    angles = phases.astype(jnp.float32) * (2.0 * math.pi / lon_total)
    cosine = jnp.cos(angles)
    sine_part = jnp.sin(angles)
    weights = jnp.where(wave_list == 0, 1.0, 2.0).astype(jnp.float32)[:, None]
    inverse = jnp.stack([weights * cosine, -(weights * sine_part)], axis=0).astype(jnp.bfloat16)
    factor = 2.0 / lon_total
    direct = jnp.stack([factor * cosine, -(factor * sine_part)], axis=0)
    direct = jnp.transpose(direct, (2, 0, 1)).astype(jnp.bfloat16)
    return (inverse, direct)


def mix_levels(temper, diverg, geopot, omega_vel, sin_lat):
    first_field = geopot + omega_vel * temper
    second_field = sin_lat[None, :, None] * omega_vel + diverg * temper
    return jnp.stack([first_field, second_field], axis=1).astype(jnp.bfloat16)


def general_body(spectral, legendre, thickness, pressure_step, wave_order, lat_order):
    wave_index = lax.axis_index("wave")
    wave_count = lax.axis_size("wave")
    local_slots = legendre.shape[0]
    grid_lats = NLAT // wave_count
    my_waves = lax.dynamic_slice(wave_order, (wave_index * local_slots,), (local_slots,))
    row_ids = jnp.arange(M, dtype=jnp.int32)
    in_triangle = row_ids[None, :] < (M - my_waves)[:, None]
    masked_leg = jnp.where(in_triangle[:, None, :], legendre, jnp.zeros((), jnp.bfloat16))
    fourier = jnp.einsum(
        "lfcsk,sqk->lfcsq",
        lax.all_gather(spectral, "lev", axis=0, tiled=True),
        masked_leg,
        preferred_element_type=jnp.float32,
    ).astype(jnp.bfloat16)
    level_split = lax.all_to_all(fourier, "lev", split_axis=0, concat_axis=4, tiled=True)
    inverse_table, forward_legendre_table = wave_tables(wave_order, NLON)
    grid_vals = jnp.einsum(
        "lfcsq,cst->lfqt",
        lax.all_to_all(level_split, "wave", split_axis=4, concat_axis=3, tiled=True),
        inverse_table,
        preferred_element_type=jnp.float32,
    )
    lat_ids = lax.dynamic_slice(lat_order, (wave_index * grid_lats,), (grid_lats,))
    angles = math.pi * (lat_ids.astype(jnp.float32) + 0.75) / (NLAT + 0.5)
    sin_lat = jnp.cos(angles)
    cos_lat = jnp.sin(angles)
    columns = lax.all_to_all(grid_vals, "lev", split_axis=3, concat_axis=0, tiled=True)
    temper = columns[:, 0]
    diverg = columns[:, 1]
    geopot = jnp.flip(jnp.cumsum(jnp.flip(thickness[:, None, None] * temper, 0), axis=0), 0)
    omega_vel = -jnp.cumsum(pressure_step[:, None, None] * diverg, axis=0)
    tend_cols = mix_levels(temper, diverg, geopot, omega_vel, sin_lat)
    tendency_field = lax.all_to_all(tend_cols, "lev", split_axis=0, concat_axis=3, tiled=True)
    returned_grid_values = (
        jnp.einsum(
            "opgu,ukh->opkhg",
            tendency_field,
            forward_legendre_table,
            preferred_element_type=jnp.float32,
        )
        * cos_lat
    ).astype(jnp.bfloat16)
    band_vals = lax.all_to_all(
        lax.all_to_all(returned_grid_values, "wave", split_axis=3, concat_axis=4, tiled=True),
        "lev",
        split_axis=4,
        concat_axis=0,
        tiled=True,
    )
    summed = lax.psum_scatter(
        jnp.einsum("lfcsq,sqk->lfcsk", band_vals, masked_leg, preferred_element_type=jnp.float32),
        "lev",
        scatter_dimension=0,
        tiled=True,
    )
    return summed


LANES = 128
ROWS = 640
GROUP = 8
UNROLL = 8
VMEM_LIMIT = 48 * 1024 * 1024


def placed(rows, cols, row_start, col_start, count):
    r = lax.broadcasted_iota(jnp.int32, (rows, cols), 0)
    c = lax.broadcasted_iota(jnp.int32, (rows, cols), 1)
    hit = (r - row_start == c - col_start) & (c >= col_start) & (c < col_start + count)
    return jnp.where(hit, 1.0, 0.0).astype(jnp.bfloat16)


def whole(a):
    return pl.BlockSpec(a.shape, lambda i, n=len(a.shape): (0,) * n)


def greet(nw, wave, lev):
    barrier = pltpu.get_barrier_semaphore()

    @pl.loop(1, nw)
    def _(i):
        pl.semaphore_signal(barrier, inc=1, device_id={"wave": lax.rem(wave + i, nw)}, device_id_type=pl.DeviceIdType.MESH)

    pl.semaphore_signal(barrier, inc=1, device_id={"lev": 1 - lev}, device_id_type=pl.DeviceIdType.MESH)
    pl.semaphore_wait(barrier, nw)


def to_wave(src, dst, slot, target, sends, recvs, i):
    return pltpu.make_async_remote_copy(
        src_ref=src.at[target],
        dst_ref=dst.at[slot],
        send_sem=sends.at[i],
        recv_sem=recvs.at[i],
        device_id={"wave": target},
        device_id_type=pl.DeviceIdType.MESH,
    )


def to_lev(src, dst, lev, send, recv):
    return pltpu.make_async_remote_copy(
        src_ref=src, dst_ref=dst, send_sem=send, recv_sem=recv, device_id={"lev": 1 - lev}, device_id_type=pl.DeviceIdType.MESH
    )


def start_exchange(nw, wave, src, dst, sends, recvs, local):
    @pl.loop(0, nw - 1)
    def _(j):
        i = nw // 2 + (1 - 2 * lax.rem(j, 2)) * ((j + 1) // 2)
        to_wave(src, dst, wave, lax.rem(wave + i, nw), sends, recvs, i).start()

    pltpu.make_async_copy(src.at[wave], dst.at[wave], local).start()


def wait_arrivals(nw, wave, src, dst, sends, recvs, local):
    pltpu.make_async_copy(src.at[wave], dst.at[wave], local).wait()

    @pl.loop(1, nw)
    def _(i):
        to_wave(src, dst, lax.rem(wave + nw - i, nw), lax.rem(wave + i, nw), sends, recvs, i).wait_recv()


def wait_sends(nw, wave, src, dst, sends, recvs):
    @pl.loop(1, nw)
    def _(i):
        to_wave(src, dst, wave, lax.rem(wave + i, nw), sends, recvs, i).wait_send()


def fill_tables(waves, cos_ref, sin_ref, row_ref):
    turn = 2.0 * math.pi / NLON

    def angle(times):
        phase = waves * times
        return (phase - NLON * jnp.floor((phase + 0.5) * (1.0 / NLON))) * turn

    inner = angle(lax.broadcasted_iota(jnp.int32, cos_ref.shape, 0).astype(jnp.float32))
    cos_ref[...] = jnp.cos(inner)
    sin_ref[...] = jnp.sin(inner)
    blocks = row_ref.shape[1]
    outer = angle(lax.broadcasted_iota(jnp.int32, row_ref.shape[1:], 0).astype(jnp.float32) * float(LANES))
    cosine, sine = jnp.cos(outer), jnp.sin(outer)
    imaginary = lax.broadcasted_iota(jnp.int32, cosine.shape, 1) // GROUP % 2 == 1
    row_ref[0] = jnp.where(imaginary, -sine, cosine)
    row_ref[1] = jnp.where(imaginary, cosine, sine)


def overlaps(lats, nw):
    return [
        (d, b, max(lats * d, LANES * b), min(lats * (d + 1), LANES * (b + 1)))
        for d in range(nw)
        for b in range(lats * d // LANES, (lats * (d + 1) - 1) // LANES + 1)
    ]


def inverse_legendre_kernel(slots, lats, lv, nw, *refs):
    wave_ref, lane_wave_ref, own, leg_ref, out, cos_ref, sin_ref, row_ref = refs[:8]
    other, sent, cut, held, sels, lev_send, lev_recv, sends, recvs, local = refs[8:]
    step = pl.program_id(0)
    wave, lev = lax.axis_index("wave"), lax.axis_index("lev")
    tiles = cut.shape[0]
    rows = 8 * lv
    n = GROUP
    count = slots // n
    per_group = n // UNROLL

    @pl.when(step == 0)
    def _():
        greet(nw, wave, lev)
        for g in range(count):
            to_lev(own.at[g], other.at[g], lev, lev_send.at[g], lev_recv.at[g]).start()
        for i, (d, b, first, last) in enumerate(overlaps(lats, nw)):
            for l in range(lv):
                sels[i, l * LANES : (l + 1) * LANES, :] = placed(
                    LANES, LANES, first - LANES * b, lats * l + first - lats * d, last - first
                )

    @pl.when(lax.rem(step, per_group) == 0)
    def _():
        g = step // per_group
        to_lev(own.at[g], other.at[g], lev, lev_send.at[g], lev_recv.at[g]).wait()
        for b in range(tiles):
            lanes = slice(b * LANES, (b + 1) * LANES)
            mine = own[g, :, lanes].astype(jnp.float32)
            theirs = other[g, :, lanes].astype(jnp.float32)
            for a in range(4 * lv):
                x, y = mine[a * n : (a + 1) * n], theirs[a * n : (a + 1) * n]
                for half in range(2):
                    top = ((a // 2 * 2 + half) * 2 + a % 2) * n
                    cut[b, top : top + n, :] = jnp.where(lev == half, x, y)

    total = None
    for j in range(UNROLL):
        s = lax.rem(step, per_group) * UNROLL + j
        m = wave_ref[wave * slots + step * UNROLL + j]
        x = jnp.concatenate([cut[b, pl.ds(s, rows, stride=n), :] for b in range(tiles)], axis=1)
        k = lax.broadcasted_iota(jnp.int32, x.shape, 1)
        x = jnp.where(k < M - m, x * jnp.where(m == 0, 1.0, 2.0), 0.0)
        x = jnp.concatenate([x if i == j else jnp.zeros_like(x) for i in range(UNROLL)], axis=0).astype(jnp.bfloat16)
        part = lax.dot_general(leg_ref[j], x, (((1,), (1,)), ((), ())), preferred_element_type=jnp.float32)
        total = part if total is None else total + part
    y = total.T
    blocks = y.shape[1] // LANES
    for j in range(UNROLL):
        s = lax.rem(step, per_group) * UNROLL + j
        for l in range(lv):
            for b in range(blocks):
                r = rows * j + 8 * l
                held[l * blocks + b, pl.ds(s, 8, stride=n), :] = y[r : r + 8, b * LANES : (b + 1) * LANES]

    @pl.when(lax.rem(step, per_group) == per_group - 1)
    def _():
        g = step // per_group
        packed = [jnp.concatenate([held[l * blocks + b] for l in range(lv)], axis=1).astype(jnp.bfloat16) for b in range(blocks)]
        totals = [None] * nw
        for i, (d, b, _, _) in enumerate(overlaps(lats, nw)):
            part = jnp.dot(packed[b], sels[i], preferred_element_type=jnp.float32)
            totals[d] = part if totals[d] is None else totals[d] + part
        for d in range(nw):
            sent[g, d] = totals[d].astype(jnp.bfloat16)
        start_exchange(nw, wave, sent.at[g], out.at[g], sends.at[g], recvs.at[g], local.at[g])

    @pl.when(step == slots // UNROLL - 1)
    def _():
        fill_tables(lane_wave_ref[...], cos_ref, sin_ref, row_ref)

        @pl.loop(0, count)
        def _(g):
            wait_arrivals(nw, wave, sent.at[g], out.at[g], sends.at[g], recvs.at[g], local.at[g])
            wait_sends(nw, wave, sent.at[g], out.at[g], sends.at[g], recvs.at[g])


def inverse_legendre(wave_order, lane_waves, own, legendre, lv, nw):
    slots, band, rows = legendre.shape
    lats = band // nw
    count = slots // GROUP
    waves = lane_waves.shape[1]
    block = jax.ShapeDtypeStruct((count, nw, 8 * GROUP, LANES), jnp.bfloat16)
    base = jax.ShapeDtypeStruct((LANES, waves), jnp.float32)
    row = jax.ShapeDtypeStruct((2, NLON // 2 // LANES, waves), jnp.float32)
    return pl.pallas_call(
        lambda *refs: inverse_legendre_kernel(slots, lats, lv, nw, *refs),
        grid=(slots // UNROLL,),
        in_specs=[
            pl.BlockSpec(memory_space=pltpu.SMEM),
            whole(lane_waves),
            whole(own),
            pl.BlockSpec((UNROLL, band, rows), lambda s: (s, 0, 0)),
        ],
        out_specs=[pl.BlockSpec(memory_space=pl.ANY), whole(base), whole(base), whole(row)],
        out_shape=[block, base, base, row],
        scratch_shapes=[
            pltpu.VMEM(own.shape, own.dtype),
            pltpu.VMEM(block.shape, block.dtype),
            pltpu.VMEM((rows // LANES, 8 * lv * GROUP, LANES), jnp.float32),
            pltpu.VMEM((lv * band // LANES, 8 * GROUP, LANES), jnp.float32),
            pltpu.VMEM((len(overlaps(lats, nw)), lv * LANES, LANES), jnp.bfloat16),
            pltpu.SemaphoreType.DMA((count,)),
            pltpu.SemaphoreType.DMA((count,)),
            pltpu.SemaphoreType.DMA((count, nw)),
            pltpu.SemaphoreType.DMA((count, nw)),
            pltpu.SemaphoreType.DMA((count,)),
        ],
        compiler_params=pltpu.CompilerParams(vmem_limit_bytes=VMEM_LIMIT, collective_id=0, has_side_effects=True),
        cost_estimate=pl.CostEstimate(flops=2 * slots * band * rows * 256, bytes_accessed=2 * slots * band * rows, transcendentals=0),
        name="inverse_legendre",
    )(wave_order, lane_waves, own, legendre)


def grid_kernel(steps, factor, lats, lv, *refs):
    thick_ref, press_ref, lat_ref, recv, cos_ref, sin_ref, row_ref, sign_ref, down_ref, up_ref, out, operand, total, signs, lane_ref = refs
    i = pl.program_id(0)
    half = recv.shape[2] // 4
    waves = operand.shape[0]

    @pl.when(i == 0)
    def _():
        lane = lax.broadcasted_iota(jnp.int32, (8, 2 * LANES), 1)
        level = lane // LANES * lv + lane % LANES // lats
        thick = press = jnp.zeros(lane.shape, jnp.float32)
        for l in range(2 * lv):
            thick = jnp.where(level == l, thick_ref[l], thick)
            press = jnp.where(level == l, press_ref[l], press)
        top = (lax.axis_index("lev") * lax.axis_size("wave") + lax.axis_index("wave")) * lats
        lat = jnp.zeros(lane.shape, jnp.int32)
        for q in range(lats):
            lat = jnp.where(lane % LANES % lats == q, lat_ref[top + q], lat)
        angle = math.pi * (lat.astype(jnp.float32) + 0.75) / (NLAT + 0.5)
        for at, row in enumerate((thick, press, jnp.cos(angle), jnp.sin(angle))):
            lane_ref[at : at + 1, :] = row[0:1, :]
        signs[...] = jnp.broadcast_to(sign_ref[...], (LANES, waves)).T
        for j in range(4):
            block = recv[:, :, j * half : (j + 1) * half, :].reshape(waves, LANES)
            operand[:, j * LANES : (j + 1) * LANES] = block
            operand[:, (4 + j) * LANES : (5 + j) * LANES] = (block.astype(jnp.float32) * signs[...]).astype(jnp.bfloat16)

    parts = []
    for u in range(ROWS // LANES):
        at = i * (ROWS // LANES) + u
        parts.append(cos_ref[...] * row_ref[0, pl.ds(at, 1), :] - sin_ref[...] * row_ref[1, pl.ds(at, 1), :])
    table = jnp.concatenate(parts, axis=0)

    def level_sum(x, matrix):
        high = x.astype(jnp.bfloat16)
        low = (x - high.astype(jnp.float32)).astype(jnp.bfloat16)
        return jnp.dot(high, matrix, preferred_element_type=jnp.float32) + jnp.dot(low, matrix, preferred_element_type=jnp.float32)

    values = jnp.dot(table.astype(jnp.bfloat16), operand[...], preferred_element_type=jnp.float32)
    tendency = []
    for side in range(2):
        temper = values[:, 4 * LANES * side : 4 * LANES * side + 2 * LANES]
        diverg = values[:, 4 * LANES * side + 2 * LANES : 4 * LANES * (side + 1)]
        geopot = level_sum(temper * lane_ref[0:1, :], up_ref[...])
        omega = -level_sum(diverg * lane_ref[1:2, :], down_ref[...])
        tendency.append((geopot + omega * temper).astype(jnp.bfloat16))
        tendency.append((lane_ref[2:3, :] * omega + diverg * temper).astype(jnp.bfloat16))
    tendency = jnp.concatenate(tendency, axis=1)
    part = lax.dot_general((table * factor).astype(jnp.bfloat16), tendency, (((0,), (0,)), ((), ())), preferred_element_type=jnp.float32)

    @pl.when(i == 0)
    def _():
        total[...] = part

    @pl.when(i > 0)
    def _():
        total[...] += part

    @pl.when(i == steps - 1)
    def _():
        for j in range(4):
            scale = lane_ref[3:4, j % 2 * LANES : (j % 2 + 1) * LANES]
            block = total[:, j * LANES : (j + 1) * LANES] + signs[...] * total[:, (4 + j) * LANES : (5 + j) * LANES]
            block = (block * scale).astype(jnp.bfloat16)
            out[:, :, j * half : (j + 1) * half, :] = block.reshape(recv.shape[0], recv.shape[1], half, LANES)


def grid_space(scalars, lats, lv, *args):
    steps = NLON // 2 // ROWS
    waves = args[1].shape[1]
    recv = args[0]
    return pl.pallas_call(
        lambda *refs: grid_kernel(steps, 2.0 / NLON, lats, lv, *refs),
        grid=(steps,),
        in_specs=[pl.BlockSpec(memory_space=pltpu.SMEM)] * len(scalars) + [whole(a) for a in args],
        out_specs=whole(recv),
        out_shape=jax.ShapeDtypeStruct(recv.shape, recv.dtype),
        scratch_shapes=[
            pltpu.VMEM((waves, 8 * LANES), jnp.bfloat16),
            pltpu.VMEM((waves, 8 * LANES), jnp.float32),
            pltpu.VMEM((waves, LANES), jnp.float32),
            pltpu.VMEM((8, 2 * LANES), jnp.float32),
        ],
        compiler_params=pltpu.CompilerParams(vmem_limit_bytes=VMEM_LIMIT),
        cost_estimate=pl.CostEstimate(flops=4 * NLON * waves * 4 * LANES, bytes_accessed=8 * waves * LANES, transcendentals=0),
        name="grid_space",
    )(*scalars, *args)


def direct_legendre_kernel(slots, lats, lv, nw, *refs):
    wave_ref, back, leg_ref, out_ref, arrived, partial, land, held, cut, sels, lev_send, lev_recv, sends, recvs, local = refs
    step = pl.program_id(0)
    wave, lev = lax.axis_index("wave"), lax.axis_index("lev")
    blocks = leg_ref.shape[1] // LANES
    tiles = cut.shape[0]
    n = GROUP
    count = slots // n
    per_group = n // UNROLL

    @pl.when(step == 0)
    def _():
        greet(nw, wave, lev)

        @pl.loop(0, count)
        def _(g):
            start_exchange(nw, wave, back.at[g], arrived.at[g], sends.at[g], recvs.at[g], local.at[g])

        for i, (d, b, first, last) in enumerate(overlaps(lats, nw)):
            for l in range(lv):
                sels[i, :, l * LANES : (l + 1) * LANES] = placed(
                    LANES, LANES, lats * l + first - lats * d, first - LANES * b, last - first
                )

    @pl.when(lax.rem(step, per_group) == 0)
    def _():
        g = step // per_group
        wait_arrivals(nw, wave, back.at[g], arrived.at[g], sends.at[g], recvs.at[g], local.at[g])
        totals = [None] * blocks
        for i, (d, b, _, _) in enumerate(overlaps(lats, nw)):
            part = jnp.dot(arrived[g, d], sels[i], preferred_element_type=jnp.float32)
            totals[b] = part if totals[b] is None else totals[b] + part
        for b in range(blocks):
            for l in range(lv):
                held[l * blocks + b] = totals[b][:, l * LANES : (l + 1) * LANES]

    for j in range(UNROLL):
        s = lax.rem(step, per_group) * UNROLL + j
        x = jnp.concatenate(
            [jnp.concatenate([held[l * blocks + b, pl.ds(s, 8, stride=n), :] for b in range(blocks)], axis=1) for l in range(lv)], axis=0
        ).astype(jnp.bfloat16)
        y = jnp.dot(x, leg_ref[j], preferred_element_type=jnp.float32)
        k = lax.broadcasted_iota(jnp.int32, y.shape, 1)
        y = jnp.where(k < M - wave_ref[wave * slots + step * UNROLL + j], y, 0.0)
        for b in range(tiles):
            cut[b, pl.ds(s, 8 * lv, stride=n), :] = y[:, b * LANES : (b + 1) * LANES]

    @pl.when(lax.rem(step, per_group) == per_group - 1)
    def _():
        g = step // per_group
        start = pl.multiple_of(g * n, n)
        for b in range(tiles):
            lanes = slice(b * LANES, (b + 1) * LANES)
            theirs = []
            for a in range(4 * lv):
                x, y = [cut[b, pl.ds(((a // 2 * 2 + half) * 2 + a % 2) * n, n), :] for half in range(2)]
                theirs.append(jnp.where(lev == 0, y, x))
                out_ref[pl.ds(a * slots + start, n), lanes] = jnp.where(lev == 0, x, y)
            partial[g, :, lanes] = jnp.concatenate(theirs, axis=0).astype(jnp.bfloat16)
        to_lev(partial.at[g], land.at[g], lev, lev_send.at[g], lev_recv.at[g]).start()

    @pl.when(step == slots // UNROLL - 1)
    def _():
        @pl.loop(0, count)
        def _(g):
            wait_sends(nw, wave, back.at[g], arrived.at[g], sends.at[g], recvs.at[g])

        for g in range(count):
            to_lev(partial.at[g], land.at[g], lev, lev_send.at[g], lev_recv.at[g]).wait()
            for b in range(tiles):
                lanes = slice(b * LANES, (b + 1) * LANES)
                theirs = land[g, :, lanes].astype(jnp.float32)
                for a in range(4 * lv):
                    out_ref[a * slots + g * n : a * slots + (g + 1) * n, lanes] += theirs[a * n : (a + 1) * n]


def direct_legendre(wave_order, back, legendre, lv):
    slots, band, rows = legendre.shape
    nw = back.shape[1]
    lats = band // nw
    count = slots // GROUP
    share = pltpu.VMEM((count, 4 * lv * GROUP, rows), jnp.bfloat16)
    return pl.pallas_call(
        lambda *refs: direct_legendre_kernel(slots, lats, lv, nw, *refs),
        grid=(slots // UNROLL,),
        in_specs=[
            pl.BlockSpec(memory_space=pltpu.SMEM),
            pl.BlockSpec(memory_space=pl.ANY),
            pl.BlockSpec((UNROLL, band, rows), lambda s: (s, 0, 0)),
        ],
        out_specs=pl.BlockSpec((4 * lv * slots, rows), lambda s: (0, 0)),
        out_shape=jax.ShapeDtypeStruct((4 * lv * slots, rows), jnp.float32),
        scratch_shapes=[
            pltpu.VMEM(back.shape, back.dtype),
            share,
            share,
            pltpu.VMEM((lv * band // LANES, 8 * GROUP, LANES), jnp.float32),
            pltpu.VMEM((rows // LANES, 8 * lv * GROUP, LANES), jnp.float32),
            pltpu.VMEM((len(overlaps(lats, nw)), LANES, lv * LANES), jnp.bfloat16),
            pltpu.SemaphoreType.DMA((count,)),
            pltpu.SemaphoreType.DMA((count,)),
            pltpu.SemaphoreType.DMA((count, nw)),
            pltpu.SemaphoreType.DMA((count, nw)),
            pltpu.SemaphoreType.DMA((count,)),
        ],
        compiler_params=pltpu.CompilerParams(vmem_limit_bytes=VMEM_LIMIT, collective_id=1, has_side_effects=True),
        cost_estimate=pl.CostEstimate(flops=2 * slots * band * rows * 256, bytes_accessed=2 * slots * band * rows, transcendentals=0),
        name="direct_legendre",
    )(wave_order, back, legendre)


def body(spectral, legendre, thickness, pressure_step, wave_order, lat_order):
    nw = lax.axis_size("wave")
    slots, band, rows = legendre.shape
    lats = band // nw
    lv = spectral.shape[0]
    count = slots // GROUP
    own = spectral.reshape(4 * lv, count, GROUP, rows).swapaxes(0, 1).reshape(count, 4 * lv * GROUP, rows)
    by_group = wave_order.reshape(nw, count, 1, GROUP).swapaxes(0, 1)
    lane_waves = jnp.broadcast_to(by_group, (count, nw, 2, GROUP)).reshape(1, -1)
    signs = (1 - 2 * (lane_waves % 2)).astype(jnp.float32)
    lane_waves = lane_waves.astype(jnp.float32)

    place = jnp.arange(2 * LANES)
    valid = place % LANES < lv * lats
    level = place // LANES * lv + place % LANES // lats
    lat = place % LANES % lats
    same = (lat[:, None] == lat[None, :]) & valid[:, None] & valid[None, :]
    down = (same & (level[:, None] <= level[None, :])).astype(jnp.bfloat16)
    up = (same & (level[:, None] >= level[None, :])).astype(jnp.bfloat16)

    recv, cos_base, sin_base, row_table = inverse_legendre(wave_order, lane_waves, own, legendre, lv, nw)
    back = grid_space((thickness, pressure_step, lat_order), lats, lv, recv, cos_base, sin_base, row_table, signs, down, up)
    out = direct_legendre(wave_order, back, legendre, lv)
    return out.reshape(lv, 2, 2, slots, rows)


def solution(mesh):
    nw, nl = mesh.shape["wave"], mesh.shape["lev"]

    def run(spectral, *rest):
        slots, lv = M // nw, spectral.shape[0] // nl
        fits = nl == 2 and NLAT % (nw * nl) == 0 and M % nw == 0 and slots % GROUP == 0 and nw % 2 == 0
        fits = fits and M % LANES == 0 and lv * (NLAT // (nw * nl)) <= LANES and (NLAT // nl) % LANES == 0
        in_specs = (P("lev", None, None, "wave", None), P("wave", "lev", None), P(), P(), P(), P())
        out_specs = P("lev", None, None, "wave", None)
        chosen = body if fits else general_body
        return jax.shard_map(chosen, mesh=mesh, in_specs=in_specs, out_specs=out_specs, check_vma=False)(spectral, *rest)

    return run
```

```python
import math

import jax
import jax.numpy as jnp
from jax import lax
from jax.experimental import pallas as pl
from jax.experimental.pallas import tpu as pltpu
from jax.sharding import PartitionSpec as P

M = 640
NLAT = 1280
NLON = 2560


def wave_tables(wave_list, lon_total):
    lon_ids = jnp.arange(lon_total, dtype=jnp.int32)
    phases = wave_list[:, None] * lon_ids[None, :] % lon_total
    angles = phases.astype(jnp.float32) * (2.0 * math.pi / lon_total)
    cosine = jnp.cos(angles)
    sine_part = jnp.sin(angles)
    weights = jnp.where(wave_list == 0, 1.0, 2.0).astype(jnp.float32)[:, None]
    inverse = jnp.stack([weights * cosine, -(weights * sine_part)], axis=0).astype(jnp.bfloat16)
    factor = 2.0 / lon_total
    direct = jnp.stack([factor * cosine, -(factor * sine_part)], axis=0)
    direct = jnp.transpose(direct, (2, 0, 1)).astype(jnp.bfloat16)
    return (inverse, direct)


def mix_levels(temper, diverg, geopot, omega_vel, sin_lat):
    first_field = geopot + omega_vel * temper
    second_field = sin_lat[None, :, None] * omega_vel + diverg * temper
    return jnp.stack([first_field, second_field], axis=1).astype(jnp.bfloat16)


def general_body(spectral, legendre, thickness, pressure_step, wave_order, lat_order):
    wave_index = lax.axis_index("wave")
    wave_count = lax.axis_size("wave")
    local_slots = legendre.shape[0]
    grid_lats = NLAT // wave_count
    my_waves = lax.dynamic_slice(wave_order, (wave_index * local_slots,), (local_slots,))
    row_ids = jnp.arange(M, dtype=jnp.int32)
    in_triangle = row_ids[None, :] < (M - my_waves)[:, None]
    masked_leg = jnp.where(in_triangle[:, None, :], legendre, jnp.zeros((), jnp.bfloat16))
    fourier = jnp.einsum(
        "lfcsk,sqk->lfcsq",
        lax.all_gather(spectral, "lev", axis=0, tiled=True),
        masked_leg,
        preferred_element_type=jnp.float32,
    ).astype(jnp.bfloat16)
    level_split = lax.all_to_all(fourier, "lev", split_axis=0, concat_axis=4, tiled=True)
    inverse_table, forward_legendre_table = wave_tables(wave_order, NLON)
    grid_vals = jnp.einsum(
        "lfcsq,cst->lfqt",
        lax.all_to_all(level_split, "wave", split_axis=4, concat_axis=3, tiled=True),
        inverse_table,
        preferred_element_type=jnp.float32,
    )
    lat_ids = lax.dynamic_slice(lat_order, (wave_index * grid_lats,), (grid_lats,))
    angles = math.pi * (lat_ids.astype(jnp.float32) + 0.75) / (NLAT + 0.5)
    sin_lat = jnp.cos(angles)
    cos_lat = jnp.sin(angles)
    columns = lax.all_to_all(grid_vals, "lev", split_axis=3, concat_axis=0, tiled=True)
    temper = columns[:, 0]
    diverg = columns[:, 1]
    geopot = jnp.flip(jnp.cumsum(jnp.flip(thickness[:, None, None] * temper, 0), axis=0), 0)
    omega_vel = -jnp.cumsum(pressure_step[:, None, None] * diverg, axis=0)
    tend_cols = mix_levels(temper, diverg, geopot, omega_vel, sin_lat)
    tendency_field = lax.all_to_all(tend_cols, "lev", split_axis=0, concat_axis=3, tiled=True)
    returned_grid_values = (
        jnp.einsum(
            "opgu,ukh->opkhg",
            tendency_field,
            forward_legendre_table,
            preferred_element_type=jnp.float32,
        )
        * cos_lat
    ).astype(jnp.bfloat16)
    band_vals = lax.all_to_all(
        lax.all_to_all(returned_grid_values, "wave", split_axis=3, concat_axis=4, tiled=True),
        "lev",
        split_axis=4,
        concat_axis=0,
        tiled=True,
    )
    summed = lax.psum_scatter(
        jnp.einsum("lfcsq,sqk->lfcsk", band_vals, masked_leg, preferred_element_type=jnp.float32),
        "lev",
        scatter_dimension=0,
        tiled=True,
    )
    return summed


LANES = 128
ROWS = 640
GROUP = 8
UNROLL = 8
VMEM_LIMIT = 48 * 1024 * 1024


def placed(rows, cols, row_start, col_start, count):
    r = lax.broadcasted_iota(jnp.int32, (rows, cols), 0)
    c = lax.broadcasted_iota(jnp.int32, (rows, cols), 1)
    hit = (r - row_start == c - col_start) & (c >= col_start) & (c < col_start + count)
    return jnp.where(hit, 1.0, 0.0).astype(jnp.bfloat16)


def whole(a):
    return pl.BlockSpec(a.shape, lambda i, n=len(a.shape): (0,) * n)


def greet(nw, wave, lev):
    barrier = pltpu.get_barrier_semaphore()

    @pl.loop(1, nw)
    def _(i):
        pl.semaphore_signal(barrier, inc=1, device_id={"wave": lax.rem(wave + i, nw)}, device_id_type=pl.DeviceIdType.MESH)

    pl.semaphore_signal(barrier, inc=1, device_id={"lev": 1 - lev}, device_id_type=pl.DeviceIdType.MESH)
    pl.semaphore_wait(barrier, nw)


def to_wave(src, dst, slot, target, sends, recvs, i):
    return pltpu.make_async_remote_copy(
        src_ref=src.at[target],
        dst_ref=dst.at[slot],
        send_sem=sends.at[i],
        recv_sem=recvs.at[i],
        device_id={"wave": target},
        device_id_type=pl.DeviceIdType.MESH,
    )


def to_lev(src, dst, lev, send, recv):
    return pltpu.make_async_remote_copy(
        src_ref=src, dst_ref=dst, send_sem=send, recv_sem=recv, device_id={"lev": 1 - lev}, device_id_type=pl.DeviceIdType.MESH
    )


def start_exchange(nw, wave, src, dst, sends, recvs, local):
    @pl.loop(1, nw)
    def _(i):
        to_wave(src, dst, wave, lax.rem(wave + i, nw), sends, recvs, i).start()

    pltpu.make_async_copy(src.at[wave], dst.at[wave], local).start()


def wait_arrivals(nw, wave, src, dst, sends, recvs, local):
    pltpu.make_async_copy(src.at[wave], dst.at[wave], local).wait()

    @pl.loop(1, nw)
    def _(i):
        to_wave(src, dst, lax.rem(wave + nw - i, nw), lax.rem(wave + i, nw), sends, recvs, i).wait_recv()


def wait_sends(nw, wave, src, dst, sends, recvs):
    @pl.loop(1, nw)
    def _(i):
        to_wave(src, dst, wave, lax.rem(wave + i, nw), sends, recvs, i).wait_send()


def fill_tables(waves, cos_ref, sin_ref, row_ref):
    turn = 2.0 * math.pi / NLON

    def angle(times):
        phase = waves * times
        return (phase - NLON * jnp.floor((phase + 0.5) * (1.0 / NLON))) * turn

    inner = angle(lax.broadcasted_iota(jnp.int32, cos_ref.shape, 0).astype(jnp.float32))
    cos_ref[...] = jnp.cos(inner)
    sin_ref[...] = jnp.sin(inner)
    blocks = row_ref.shape[1]
    outer = angle(lax.broadcasted_iota(jnp.int32, row_ref.shape[1:], 0).astype(jnp.float32) * float(LANES))
    cosine, sine = jnp.cos(outer), jnp.sin(outer)
    imaginary = lax.broadcasted_iota(jnp.int32, cosine.shape, 1) // GROUP % 2 == 1
    row_ref[0] = jnp.where(imaginary, -sine, cosine)
    row_ref[1] = jnp.where(imaginary, cosine, sine)


def overlaps(lats, nw):
    return [
        (d, b, max(lats * d, LANES * b), min(lats * (d + 1), LANES * (b + 1)))
        for d in range(nw)
        for b in range(lats * d // LANES, (lats * (d + 1) - 1) // LANES + 1)
    ]


def inverse_legendre_kernel(slots, lats, lv, nw, *refs):
    wave_ref, lane_wave_ref, own, leg_ref, out, cos_ref, sin_ref, row_ref = refs[:8]
    other, sent, cut, held, sels, lev_send, lev_recv, sends, recvs, local = refs[8:]
    step = pl.program_id(0)
    wave, lev = lax.axis_index("wave"), lax.axis_index("lev")
    tiles = cut.shape[0]
    rows = 8 * lv
    n = GROUP
    count = slots // n
    per_group = n // UNROLL

    @pl.when(step == 0)
    def _():
        greet(nw, wave, lev)
        for g in range(count):
            to_lev(own.at[g], other.at[g], lev, lev_send.at[g], lev_recv.at[g]).start()
        for i, (d, b, first, last) in enumerate(overlaps(lats, nw)):
            for l in range(lv):
                sels[i, l * LANES : (l + 1) * LANES, :] = placed(
                    LANES, LANES, first - LANES * b, lats * l + first - lats * d, last - first
                )

    @pl.when(lax.rem(step, per_group) == 0)
    def _():
        g = step // per_group
        to_lev(own.at[g], other.at[g], lev, lev_send.at[g], lev_recv.at[g]).wait()
        for b in range(tiles):
            lanes = slice(b * LANES, (b + 1) * LANES)
            mine = own[g, :, lanes].astype(jnp.float32)
            theirs = other[g, :, lanes].astype(jnp.float32)
            for a in range(4 * lv):
                x, y = mine[a * n : (a + 1) * n], theirs[a * n : (a + 1) * n]
                for half in range(2):
                    top = ((a // 2 * 2 + half) * 2 + a % 2) * n
                    cut[b, top : top + n, :] = jnp.where(lev == half, x, y)

    total = None
    for j in range(UNROLL):
        s = lax.rem(step, per_group) * UNROLL + j
        m = wave_ref[wave * slots + step * UNROLL + j]
        x = jnp.concatenate([cut[b, pl.ds(s, rows, stride=n), :] for b in range(tiles)], axis=1)
        k = lax.broadcasted_iota(jnp.int32, x.shape, 1)
        x = jnp.where(k < M - m, x * jnp.where(m == 0, 1.0, 2.0), 0.0)
        x = jnp.concatenate([x if i == j else jnp.zeros_like(x) for i in range(UNROLL)], axis=0).astype(jnp.bfloat16)
        part = lax.dot_general(leg_ref[j], x, (((1,), (1,)), ((), ())), preferred_element_type=jnp.float32)
        total = part if total is None else total + part
    y = total.T
    blocks = y.shape[1] // LANES
    for j in range(UNROLL):
        s = lax.rem(step, per_group) * UNROLL + j
        for l in range(lv):
            for b in range(blocks):
                r = rows * j + 8 * l
                held[l * blocks + b, pl.ds(s, 8, stride=n), :] = y[r : r + 8, b * LANES : (b + 1) * LANES]

    @pl.when(lax.rem(step, per_group) == per_group - 1)
    def _():
        g = step // per_group
        packed = [jnp.concatenate([held[l * blocks + b] for l in range(lv)], axis=1).astype(jnp.bfloat16) for b in range(blocks)]
        totals = [None] * nw
        for i, (d, b, _, _) in enumerate(overlaps(lats, nw)):
            part = jnp.dot(packed[b], sels[i], preferred_element_type=jnp.float32)
            totals[d] = part if totals[d] is None else totals[d] + part
        for d in range(nw):
            sent[g, d] = totals[d].astype(jnp.bfloat16)
        start_exchange(nw, wave, sent.at[g], out.at[g], sends.at[g], recvs.at[g], local.at[g])

    @pl.when(step == slots // UNROLL - 1)
    def _():
        fill_tables(lane_wave_ref[...], cos_ref, sin_ref, row_ref)

        @pl.loop(0, count)
        def _(g):
            wait_arrivals(nw, wave, sent.at[g], out.at[g], sends.at[g], recvs.at[g], local.at[g])
            wait_sends(nw, wave, sent.at[g], out.at[g], sends.at[g], recvs.at[g])


def inverse_legendre(wave_order, lane_waves, own, legendre, lv, nw):
    slots, band, rows = legendre.shape
    lats = band // nw
    count = slots // GROUP
    waves = lane_waves.shape[1]
    block = jax.ShapeDtypeStruct((count, nw, 8 * GROUP, LANES), jnp.bfloat16)
    base = jax.ShapeDtypeStruct((LANES, waves), jnp.float32)
    row = jax.ShapeDtypeStruct((2, NLON // 2 // LANES, waves), jnp.float32)
    return pl.pallas_call(
        lambda *refs: inverse_legendre_kernel(slots, lats, lv, nw, *refs),
        grid=(slots // UNROLL,),
        in_specs=[
            pl.BlockSpec(memory_space=pltpu.SMEM),
            whole(lane_waves),
            whole(own),
            pl.BlockSpec((UNROLL, band, rows), lambda s: (s, 0, 0)),
        ],
        out_specs=[pl.BlockSpec(memory_space=pl.ANY), whole(base), whole(base), whole(row)],
        out_shape=[block, base, base, row],
        scratch_shapes=[
            pltpu.VMEM(own.shape, own.dtype),
            pltpu.VMEM(block.shape, block.dtype),
            pltpu.VMEM((rows // LANES, 8 * lv * GROUP, LANES), jnp.float32),
            pltpu.VMEM((lv * band // LANES, 8 * GROUP, LANES), jnp.float32),
            pltpu.VMEM((len(overlaps(lats, nw)), lv * LANES, LANES), jnp.bfloat16),
            pltpu.SemaphoreType.DMA((count,)),
            pltpu.SemaphoreType.DMA((count,)),
            pltpu.SemaphoreType.DMA((count, nw)),
            pltpu.SemaphoreType.DMA((count, nw)),
            pltpu.SemaphoreType.DMA((count,)),
        ],
        compiler_params=pltpu.CompilerParams(vmem_limit_bytes=VMEM_LIMIT, collective_id=0, has_side_effects=True),
        cost_estimate=pl.CostEstimate(flops=2 * slots * band * rows * 256, bytes_accessed=2 * slots * band * rows, transcendentals=0),
        name="inverse_legendre",
    )(wave_order, lane_waves, own, legendre)


def grid_kernel(steps, factor, lats, lv, *refs):
    thick_ref, press_ref, lat_ref, recv, cos_ref, sin_ref, row_ref, sign_ref, down_ref, up_ref, out, operand, total, signs, lane_ref = refs
    i = pl.program_id(0)
    half = recv.shape[2] // 4
    waves = operand.shape[0]

    @pl.when(i == 0)
    def _():
        lane = lax.broadcasted_iota(jnp.int32, (8, 2 * LANES), 1)
        level = lane // LANES * lv + lane % LANES // lats
        thick = press = jnp.zeros(lane.shape, jnp.float32)
        for l in range(2 * lv):
            thick = jnp.where(level == l, thick_ref[l], thick)
            press = jnp.where(level == l, press_ref[l], press)
        top = (lax.axis_index("lev") * lax.axis_size("wave") + lax.axis_index("wave")) * lats
        lat = jnp.zeros(lane.shape, jnp.int32)
        for q in range(lats):
            lat = jnp.where(lane % LANES % lats == q, lat_ref[top + q], lat)
        angle = math.pi * (lat.astype(jnp.float32) + 0.75) / (NLAT + 0.5)
        for at, row in enumerate((thick, press, jnp.cos(angle), jnp.sin(angle))):
            lane_ref[at : at + 1, :] = row[0:1, :]
        signs[...] = jnp.broadcast_to(sign_ref[...], (LANES, waves)).T
        for j in range(4):
            block = recv[:, :, j * half : (j + 1) * half, :].reshape(waves, LANES)
            operand[:, j * LANES : (j + 1) * LANES] = block
            operand[:, (4 + j) * LANES : (5 + j) * LANES] = (block.astype(jnp.float32) * signs[...]).astype(jnp.bfloat16)

    parts = []
    for u in range(ROWS // LANES):
        at = i * (ROWS // LANES) + u
        parts.append(cos_ref[...] * row_ref[0, pl.ds(at, 1), :] - sin_ref[...] * row_ref[1, pl.ds(at, 1), :])
    table = jnp.concatenate(parts, axis=0)

    def level_sum(x, matrix):
        high = x.astype(jnp.bfloat16)
        low = (x - high.astype(jnp.float32)).astype(jnp.bfloat16)
        return jnp.dot(high, matrix, preferred_element_type=jnp.float32) + jnp.dot(low, matrix, preferred_element_type=jnp.float32)

    values = jnp.dot(table.astype(jnp.bfloat16), operand[...], preferred_element_type=jnp.float32)
    tendency = []
    for side in range(2):
        temper = values[:, 4 * LANES * side : 4 * LANES * side + 2 * LANES]
        diverg = values[:, 4 * LANES * side + 2 * LANES : 4 * LANES * (side + 1)]
        geopot = level_sum(temper * lane_ref[0:1, :], up_ref[...])
        omega = -level_sum(diverg * lane_ref[1:2, :], down_ref[...])
        tendency.append((geopot + omega * temper).astype(jnp.bfloat16))
        tendency.append((lane_ref[2:3, :] * omega + diverg * temper).astype(jnp.bfloat16))
    tendency = jnp.concatenate(tendency, axis=1)
    part = lax.dot_general((table * factor).astype(jnp.bfloat16), tendency, (((0,), (0,)), ((), ())), preferred_element_type=jnp.float32)

    @pl.when(i == 0)
    def _():
        total[...] = part

    @pl.when(i > 0)
    def _():
        total[...] += part

    @pl.when(i == steps - 1)
    def _():
        for j in range(4):
            scale = lane_ref[3:4, j % 2 * LANES : (j % 2 + 1) * LANES]
            block = total[:, j * LANES : (j + 1) * LANES] + signs[...] * total[:, (4 + j) * LANES : (5 + j) * LANES]
            block = (block * scale).astype(jnp.bfloat16)
            out[:, :, j * half : (j + 1) * half, :] = block.reshape(recv.shape[0], recv.shape[1], half, LANES)


def grid_space(scalars, lats, lv, *args):
    steps = NLON // 2 // ROWS
    waves = args[1].shape[1]
    recv = args[0]
    return pl.pallas_call(
        lambda *refs: grid_kernel(steps, 2.0 / NLON, lats, lv, *refs),
        grid=(steps,),
        in_specs=[pl.BlockSpec(memory_space=pltpu.SMEM)] * len(scalars) + [whole(a) for a in args],
        out_specs=whole(recv),
        out_shape=jax.ShapeDtypeStruct(recv.shape, recv.dtype),
        scratch_shapes=[
            pltpu.VMEM((waves, 8 * LANES), jnp.bfloat16),
            pltpu.VMEM((waves, 8 * LANES), jnp.float32),
            pltpu.VMEM((waves, LANES), jnp.float32),
            pltpu.VMEM((8, 2 * LANES), jnp.float32),
        ],
        compiler_params=pltpu.CompilerParams(vmem_limit_bytes=VMEM_LIMIT),
        cost_estimate=pl.CostEstimate(flops=4 * NLON * waves * 4 * LANES, bytes_accessed=8 * waves * LANES, transcendentals=0),
        name="grid_space",
    )(*scalars, *args)


def direct_legendre_kernel(slots, lats, lv, nw, *refs):
    wave_ref, back, leg_ref, out_ref, arrived, partial, land, held, cut, sels, lev_send, lev_recv, sends, recvs, local = refs
    step = pl.program_id(0)
    wave, lev = lax.axis_index("wave"), lax.axis_index("lev")
    blocks = leg_ref.shape[1] // LANES
    tiles = cut.shape[0]
    n = GROUP
    count = slots // n
    per_group = n // UNROLL

    @pl.when(step == 0)
    def _():
        greet(nw, wave, lev)

        @pl.loop(0, count)
        def _(g):
            start_exchange(nw, wave, back.at[g], arrived.at[g], sends.at[g], recvs.at[g], local.at[g])

        for i, (d, b, first, last) in enumerate(overlaps(lats, nw)):
            for l in range(lv):
                sels[i, :, l * LANES : (l + 1) * LANES] = placed(
                    LANES, LANES, lats * l + first - lats * d, first - LANES * b, last - first
                )

    @pl.when(lax.rem(step, per_group) == 0)
    def _():
        g = step // per_group
        wait_arrivals(nw, wave, back.at[g], arrived.at[g], sends.at[g], recvs.at[g], local.at[g])
        totals = [None] * blocks
        for i, (d, b, _, _) in enumerate(overlaps(lats, nw)):
            part = jnp.dot(arrived[g, d], sels[i], preferred_element_type=jnp.float32)
            totals[b] = part if totals[b] is None else totals[b] + part
        for b in range(blocks):
            for l in range(lv):
                held[l * blocks + b] = totals[b][:, l * LANES : (l + 1) * LANES]

    for j in range(UNROLL):
        s = lax.rem(step, per_group) * UNROLL + j
        x = jnp.concatenate(
            [jnp.concatenate([held[l * blocks + b, pl.ds(s, 8, stride=n), :] for b in range(blocks)], axis=1) for l in range(lv)], axis=0
        ).astype(jnp.bfloat16)
        y = jnp.dot(x, leg_ref[j], preferred_element_type=jnp.float32)
        k = lax.broadcasted_iota(jnp.int32, y.shape, 1)
        y = jnp.where(k < M - wave_ref[wave * slots + step * UNROLL + j], y, 0.0)
        for b in range(tiles):
            cut[b, pl.ds(s, 8 * lv, stride=n), :] = y[:, b * LANES : (b + 1) * LANES]

    @pl.when(lax.rem(step, per_group) == per_group - 1)
    def _():
        g = step // per_group
        start = pl.multiple_of(g * n, n)
        for b in range(tiles):
            lanes = slice(b * LANES, (b + 1) * LANES)
            theirs = []
            for a in range(4 * lv):
                x, y = [cut[b, pl.ds(((a // 2 * 2 + half) * 2 + a % 2) * n, n), :] for half in range(2)]
                theirs.append(jnp.where(lev == 0, y, x))
                out_ref[pl.ds(a * slots + start, n), lanes] = jnp.where(lev == 0, x, y)
            partial[g, :, lanes] = jnp.concatenate(theirs, axis=0).astype(jnp.bfloat16)
        to_lev(partial.at[g], land.at[g], lev, lev_send.at[g], lev_recv.at[g]).start()

    @pl.when(step == slots // UNROLL - 1)
    def _():
        @pl.loop(0, count)
        def _(g):
            wait_sends(nw, wave, back.at[g], arrived.at[g], sends.at[g], recvs.at[g])

        for g in range(count):
            to_lev(partial.at[g], land.at[g], lev, lev_send.at[g], lev_recv.at[g]).wait()
            for b in range(tiles):
                lanes = slice(b * LANES, (b + 1) * LANES)
                theirs = land[g, :, lanes].astype(jnp.float32)
                for a in range(4 * lv):
                    out_ref[a * slots + g * n : a * slots + (g + 1) * n, lanes] += theirs[a * n : (a + 1) * n]


def direct_legendre(wave_order, back, legendre, lv):
    slots, band, rows = legendre.shape
    nw = back.shape[1]
    lats = band // nw
    count = slots // GROUP
    share = pltpu.VMEM((count, 4 * lv * GROUP, rows), jnp.bfloat16)
    return pl.pallas_call(
        lambda *refs: direct_legendre_kernel(slots, lats, lv, nw, *refs),
        grid=(slots // UNROLL,),
        in_specs=[
            pl.BlockSpec(memory_space=pltpu.SMEM),
            pl.BlockSpec(memory_space=pl.ANY),
            pl.BlockSpec((UNROLL, band, rows), lambda s: (s, 0, 0)),
        ],
        out_specs=pl.BlockSpec((4 * lv * slots, rows), lambda s: (0, 0)),
        out_shape=jax.ShapeDtypeStruct((4 * lv * slots, rows), jnp.float32),
        scratch_shapes=[
            pltpu.VMEM(back.shape, back.dtype),
            share,
            share,
            pltpu.VMEM((lv * band // LANES, 8 * GROUP, LANES), jnp.float32),
            pltpu.VMEM((rows // LANES, 8 * lv * GROUP, LANES), jnp.float32),
            pltpu.VMEM((len(overlaps(lats, nw)), LANES, lv * LANES), jnp.bfloat16),
            pltpu.SemaphoreType.DMA((count,)),
            pltpu.SemaphoreType.DMA((count,)),
            pltpu.SemaphoreType.DMA((count, nw)),
            pltpu.SemaphoreType.DMA((count, nw)),
            pltpu.SemaphoreType.DMA((count,)),
        ],
        compiler_params=pltpu.CompilerParams(vmem_limit_bytes=VMEM_LIMIT, collective_id=1, has_side_effects=True),
        cost_estimate=pl.CostEstimate(flops=2 * slots * band * rows * 256, bytes_accessed=2 * slots * band * rows, transcendentals=0),
        name="direct_legendre",
    )(wave_order, back, legendre)


def body(spectral, legendre, thickness, pressure_step, wave_order, lat_order):
    nw = lax.axis_size("wave")
    slots, band, rows = legendre.shape
    lats = band // nw
    lv = spectral.shape[0]
    count = slots // GROUP
    own = spectral.reshape(4 * lv, count, GROUP, rows).swapaxes(0, 1).reshape(count, 4 * lv * GROUP, rows)
    by_group = wave_order.reshape(nw, count, 1, GROUP).swapaxes(0, 1)
    lane_waves = jnp.broadcast_to(by_group, (count, nw, 2, GROUP)).reshape(1, -1)
    signs = (1 - 2 * (lane_waves % 2)).astype(jnp.float32)
    lane_waves = lane_waves.astype(jnp.float32)

    place = jnp.arange(2 * LANES)
    valid = place % LANES < lv * lats
    level = place // LANES * lv + place % LANES // lats
    lat = place % LANES % lats
    same = (lat[:, None] == lat[None, :]) & valid[:, None] & valid[None, :]
    down = (same & (level[:, None] <= level[None, :])).astype(jnp.bfloat16)
    up = (same & (level[:, None] >= level[None, :])).astype(jnp.bfloat16)

    recv, cos_base, sin_base, row_table = inverse_legendre(wave_order, lane_waves, own, legendre, lv, nw)
    back = grid_space((thickness, pressure_step, lat_order), lats, lv, recv, cos_base, sin_base, row_table, signs, down, up)
    out = direct_legendre(wave_order, back, legendre, lv)
    return out.reshape(lv, 2, 2, slots, rows)


def solution(mesh):
    nw, nl = mesh.shape["wave"], mesh.shape["lev"]

    def run(spectral, *rest):
        slots, lv = M // nw, spectral.shape[0] // nl
        fits = nl == 2 and NLAT % (nw * nl) == 0 and M % nw == 0 and slots % GROUP == 0 and nw % 2 == 0
        fits = fits and M % LANES == 0 and lv * (NLAT // (nw * nl)) <= LANES and (NLAT // nl) % LANES == 0
        in_specs = (P("lev", None, None, "wave", None), P("wave", "lev", None), P(), P(), P(), P())
        out_specs = P("lev", None, None, "wave", None)
        chosen = body if fits else general_body
        return jax.shard_map(chosen, mesh=mesh, in_specs=in_specs, out_specs=out_specs, check_vma=False)(spectral, *rest)

    return run
```
